512 devices in a mesh: req: 32 (over x, y, core), head: 16 (over z).
Axes of the slice: x: 4, y: 4, z: 16, core: 2. Of those that a mesh axis runs over, the one named last changes fastest.
Arguments:
- queries: bfloat16 [384, 64, 4096], P('req', None, 'head'), may hold values from -1.796875 to 1.796875
- key_rows: bfloat16 [384, 64, 4096], P('req', None, 'head'), may hold values from -1.796875 to 1.796875
- values: bfloat16 [384, 64, 4096], P('req', None, 'head'), may hold values from -64 to 64
- log_decay: float32 [384, 32, 64], P('req', 'head'), may hold values from -1 to 0
- state_cache: float32 [384, 32, 128, 128], P('req', 'head'), may hold values from -24 to 24
- norm_gain: float32 [4096], P('head'), may hold values from 0.1 to 1.9
- entry_slot: int32 [384], replicated, may hold values from 0 to 383, as said below
- hit_entry: int32 [384], P('req'), may hold values from -1 to 383, as said below
- write_entry: int32 [384], P('req'), may hold values from -1 to 383, as said below
Outputs:
- attended: bfloat16 [384, 64, 4096], P('req', None, 'head')
- new_cache: float32 [384, 32, 128, 128], P('req', 'head')
The draws below stay inside these ranges and needn't reach their ends.
Inputs may be any that keep to these rules, and one draw needn't show every extreme that they name: `entry_slot`: a permutation. `hit_entry`: slot s is held by index s // 12 of req; the entries named by the 12 requests of one index of req lie on different indices. `write_entry`: no entry is named twice; the entries named by the 12 requests of one index of req lie on different indices.
All inputs are finite; a program needn't handle non-finite values.
Results may differ from the reference program's by a relative error of at most 0.0048.
Values sent between devices are 32-bit elements; how exact they have to be, the bound alone decides.
A program may use at most 128 MiB of HBM per device.

```python
import math
import jax
import jax.numpy as jnp
from jax import lax

LOCAL_HEADS = 32
HDIM = 128
REQUEST_TOKENS = 64
REQ_DEV = 12
ENT_DEV = 12
REQUEST_TOTAL = 384
ENTRIES = 384
N_REQ = 32


def slot_tables(key):
    perm_key, heat_key, score_key, pick_key, miss_key, shift_key, place_key, drop_key = jax.random.split(key, 8)
    slot_of = jax.random.permutation(perm_key, ENTRIES).astype(jnp.int32)
    entry_of = jnp.argsort(slot_of).astype(jnp.int32)
    owner_heat = jax.random.randint(heat_key, (N_REQ,), 1, 9)
    owner_score = jax.random.randint(score_key, (N_REQ, N_REQ), 0, 1 << 14) * owner_heat[None, :]
    owner_score = owner_score * N_REQ + jnp.arange(N_REQ, dtype=jnp.int32)[None, :]
    ignored, owners = lax.top_k(owner_score, REQ_DEV)
    owners = owners.astype(jnp.int32)
    top_slot = slot_of[ENTRIES - 1]
    top_holder = (top_slot // ENT_DEV).astype(jnp.int32)
    row_match = owners[0] == top_holder
    top_pos = jnp.where(jnp.any(row_match), jnp.argmax(row_match), 0).astype(jnp.int32)
    owners = owners.at[0, top_pos].set(top_holder)
    within = jax.random.randint(pick_key, (N_REQ, REQ_DEV), 0, ENT_DEV).astype(jnp.int32)
    within = within.at[0, top_pos].set((top_slot % ENT_DEV).astype(jnp.int32))
    hit_slots = owners * ENT_DEV + within
    missed = jax.random.randint(miss_key, (N_REQ, REQ_DEV), 0, 16) == 0
    missed = missed.at[0, top_pos].set(False)
    hits = jnp.where(missed, -1, entry_of[hit_slots]).astype(jnp.int32)
    shift_perm = jax.random.permutation(shift_key, N_REQ).astype(jnp.int32)
    shifts = ((shift_perm[:ENT_DEV] - shift_perm[0] + N_REQ // 2) % N_REQ).astype(jnp.int32)
    place_score = jax.random.randint(place_key, (N_REQ, REQ_DEV), 0, 1 << 10) * REQ_DEV
    place_score = place_score + jnp.arange(REQ_DEV, dtype=jnp.int32)[None, :]
    write_order = jnp.argsort(place_score, axis=1)
    write_rank = jnp.argsort(write_order, axis=1).astype(jnp.int32)
    devices = jnp.arange(N_REQ, dtype=jnp.int32)[:, None]
    target = (devices + shifts[jnp.minimum(write_rank, ENT_DEV - 1)]) % N_REQ
    target_slot = target * ENT_DEV + jnp.minimum(write_rank, ENT_DEV - 1)
    dropped = jax.random.randint(drop_key, (N_REQ, REQ_DEV), 0, 16) == 0
    keep_write = (write_rank < ENT_DEV) & jnp.logical_not(dropped)
    writes = jnp.where(keep_write, entry_of[target_slot], -1).astype(jnp.int32)
    return (slot_of, hits.reshape(REQUEST_TOTAL), writes.reshape(REQUEST_TOTAL))


def draw_entry_slot(key, part):
    tables = slot_tables(key)
    return tables[0]


def draw_hit_entry(key, part):
    tables = slot_tables(key)
    return tables[1]


def draw_write_entry(key, part):
    tables = slot_tables(key)
    return tables[2]


def draw_values(key, part):
    key = jax.random.fold_in(key, 5)
    first_key = jax.random.fold_in(key, 0)
    head_rise = jnp.arange(LOCAL_HEADS, dtype=jnp.float32) / (LOCAL_HEADS - 1)
    normal_part = jnp.clip(jax.random.normal(first_key, (REQUEST_TOTAL, REQUEST_TOKENS, LOCAL_HEADS, HDIM), jnp.float32), -4.0, 4.0)
    scaled = normal_part * (3.0 ** head_rise)[None, None, :, None]
    return scaled.reshape(REQUEST_TOTAL, REQUEST_TOKENS, LOCAL_HEADS * HDIM).astype(jnp.bfloat16)


def draw_log_decay(key, part):
    key = jax.random.fold_in(key, 7)
    variety_key, gradual_decay_key, quick_decay_key, multiplier_key, spike_random_key, penalty_key = jax.random.split(key, 6)
    slow_share = 0.5
    slow_heads = jax.random.uniform(variety_key, (REQUEST_TOTAL, LOCAL_HEADS, 1)) < slow_share
    slow_rate = jax.random.uniform(gradual_decay_key, (REQUEST_TOTAL, LOCAL_HEADS, 1), jnp.float32, 0.1, 0.5) * math.log(10.0) / REQUEST_TOKENS
    fast_rate = jax.random.uniform(quick_decay_key, (REQUEST_TOTAL, LOCAL_HEADS, 1), jnp.float32, 1.0 / 50.0, 1.0 / 30.0)
    factor = jnp.exp(jax.random.uniform(multiplier_key, (REQUEST_TOTAL, 1, 1), jnp.float32, -0.35, 0.35))
    decay_speed = jnp.where(slow_heads, slow_rate, fast_rate) * factor
    spike_events = jax.random.uniform(spike_random_key, (REQUEST_TOTAL, LOCAL_HEADS, REQUEST_TOKENS)) < 2.0 / REQUEST_TOKENS
    penalty_record = jnp.log(jax.random.uniform(penalty_key, (REQUEST_TOTAL, LOCAL_HEADS, REQUEST_TOKENS), jnp.float32, 0.5, 0.8))
    return (-decay_speed + jnp.where(spike_events, penalty_record, 0.0)).astype(jnp.float32)


def levels(key, dims, shards, smallest, top_value):
    gain, own = 1.0, jax.random.fold_in(key, 6)
    for dim, shards_of in shards:
        draws = jnp.exp(jax.random.uniform(jax.random.fold_in(own, dim), (shards_of,), jnp.float32, smallest / len(shards), top_value / len(shards)))
        gain = gain * jnp.repeat(draws, dims[dim] // shards_of).reshape([-1 if axis == dim else 1 for axis in range(len(dims))])
    return gain


def centred(rng, dims, scale, bound, shards=(), held_as=jnp.bfloat16):
    drawn = jax.random.normal(rng, dims, jnp.float32) * scale
    if len(shards) > 0:
        drawn = levels(rng, dims, shards, -0.22, 0.18) * drawn
    return jnp.clip(drawn, min=-bound, max=bound).astype(held_as)


def setup_inputs(seed: int = 0) -> dict:
    keys = jax.random.split(jax.random.key(seed), 10)
    queries = centred(keys[0], (REQUEST_TOTAL, REQUEST_TOKENS, LOCAL_HEADS * HDIM), 0.3, 1.796875, ((0, 32), (2, 16)))
    key_rows = centred(keys[1], (REQUEST_TOTAL, REQUEST_TOKENS, LOCAL_HEADS * HDIM), 0.3, 1.796875, ((0, 32), (2, 16)))
    values = draw_values(jax.random.fold_in(keys[9], 71), 0)
    log_decay = draw_log_decay(jax.random.fold_in(keys[9], 71), 0)
    state_cache = centred(keys[4], (ENTRIES, LOCAL_HEADS, HDIM, HDIM), 4.0, 24.0, ((0, 32), (1, 16)), jnp.float32)
    norm_gain = jnp.clip(1.0 + 0.18 * jax.random.normal(keys[5], (LOCAL_HEADS * HDIM,), jnp.float32), 0.1, 1.9)
    entry_slot = draw_entry_slot(jax.random.fold_in(keys[9], 71), 0)
    hit_entry = draw_hit_entry(jax.random.fold_in(keys[9], 71), 0)
    write_entry = draw_write_entry(jax.random.fold_in(keys[9], 71), 0)
    return {"queries": queries, "key_rows": key_rows, "values": values, "log_decay": log_decay, "state_cache": state_cache, "norm_gain": norm_gain, "entry_slot": entry_slot, "hit_entry": hit_entry, "write_entry": write_entry}


def request_pass(operands, state_cache, norm_gain):
    query_rows, key_block, value_block, gsum, slot, present = operands
    length = query_rows.shape[0]
    head_count = gsum.shape[0]
    head_size = query_rows.shape[1] // head_count
    query_float = query_rows.astype(jnp.float32).reshape(length, head_count, head_size)
    key_float = key_block.astype(jnp.float32).reshape(length, head_count, head_size)
    value_float = value_block.astype(jnp.float32).reshape(length, head_count, head_size)
    prefix = lax.dynamic_index_in_dim(state_cache, slot, 0, keepdims=False) * present
    prefix_high = prefix.astype(jnp.bfloat16)
    prefix_high = lax.optimization_barrier(prefix_high).astype(jnp.float32)
    prefix_low = (prefix - prefix_high).astype(jnp.bfloat16).astype(jnp.float32)
    scores = jnp.einsum('thd,shd->hts', query_float, key_float)
    gap_sums = gsum[:, :, None] - gsum[:, None, :]
    causal = jnp.arange(length)[:, None] >= jnp.arange(length)[None, :]
    weights = (scores * jnp.where(causal, jnp.exp(jnp.minimum(gap_sums, 0.0)), 0.0)).astype(jnp.bfloat16)
    weights = lax.optimization_barrier(weights).astype(jnp.float32)
    local_part = jnp.einsum('hts,shd->thd', weights, value_float)
    carried = jnp.einsum('thi,hij->thj', query_float, prefix_high) + jnp.einsum('thi,hij->thj', query_float, prefix_low)
    carried = carried * jnp.exp(gsum).T[:, :, None]
    heads_out = (local_part + carried).reshape(length, head_count * head_size)
    inv_rms = lax.rsqrt(lax.optimization_barrier(jnp.mean(heads_out * heads_out, axis=1, keepdims=True)) + 1e-06)
    attended = (heads_out * inv_rms * norm_gain).astype(jnp.bfloat16)
    tail_decay = jnp.exp(gsum[:, -1:] - gsum).T
    weighted_keys = (key_float * tail_decay[:, :, None]).astype(jnp.bfloat16)
    weighted_keys = lax.optimization_barrier(weighted_keys).astype(jnp.float32)
    final_state = jnp.exp(gsum[:, -1])[:, None, None] * prefix + jnp.einsum('shi,shj->hij', weighted_keys, value_float)
    return (attended, final_state)

def reference(queries, key_rows, values, log_decay, state_cache, norm_gain, entry_slot, hit_entry, write_entry):
    gsum = jnp.cumsum(log_decay, axis=2)
    hit_slot = jnp.where(hit_entry >= 0, entry_slot[jnp.maximum(hit_entry, 0)], 0).astype(jnp.int32)
    present = (hit_entry >= 0).astype(jnp.float32)
    attended, finals = lax.map(lambda operands: request_pass(operands, state_cache, norm_gain), (queries, key_rows, values, gsum, hit_slot, present))
    write_slot = jnp.where(write_entry >= 0, entry_slot[jnp.maximum(write_entry, 0)], ENTRIES).astype(jnp.int32)
    new_cache = state_cache.at[write_slot].set(finals, mode='drop')
    return (attended, new_cache)
```

```python
import functools

import jax
import jax.numpy as jnp
from jax import lax
from jax.experimental import pallas as pl
from jax.experimental.pallas import tpu as pltpu
from jax.sharding import PartitionSpec as P

MESH = pl.DeviceIdType.MESH
F32 = jnp.float32
BF16 = jnp.bfloat16
LANES = 128
HIT, WRITE = 0, 16


def nt(a, b, **kw):
    return lax.dot_general(a, b, (((1,), (1,)), ((), ())), preferred_element_type=F32, **kw)


def tn(a, b):
    return lax.dot_general(a, b, (((0,), (0,)), ((), ())), preferred_element_type=F32)


def kernel(
    n, nz, entry_slot, hit_entry, write_entry, log_decay, queries, key_rows, values, gain, cache,
    attended, new_cache,
    pieces, kv_pieces, kv, hit_pieces, new_pieces, prefix, heads, decay_cols, own_slots, slots,
    own_decay, decays, inverse, own_squares, squares, slots_s, decays_s, inverse_s,
    slot_send, slot_recv, decay_send, decay_recv, cache_send, cache_recv, kv_send, kv_recv,
    hit_send, hit_recv, new_send, new_recv, square_send, square_recv, local_sem,
):
    count, length, width = queries.shape
    head_count = log_decay.shape[1]
    size = width // head_count
    rows = cache.shape[1] // n
    me, z = lax.axis_index("req"), lax.axis_index("head")

    def peer_of(d):
        x, y, c = me // 8, (me // 2) % 4, me % 2
        return ((x + d // 8) % 4) * 8 + ((y + (d // 2) % 4) % 4) * 2 + (c + d % 2) % 2

    def each_peer(act):
        def step(d, carry):
            act(d, peer_of(d))
            return carry

        lax.fori_loop(1, n, step, 0)

    def each_z(act):
        def step(d, carry):
            act(d, lax.rem(z + d, nz))
            return carry

        lax.fori_loop(1, nz, step, 0)

    def remote(src, dst, send, recv, device):
        return pltpu.make_async_remote_copy(
            src_ref=src, dst_ref=dst, send_sem=send, recv_sem=recv, device_id=device, device_id_type=MESH
        )

    def part(ref, device):
        return ref.at[pl.ds(device * count, count)]

    def strip(ref, device):
        return ref.at[:, pl.ds(pl.multiple_of(device * rows, rows), rows), :]

    def slot_copy(d, peer):
        return remote(own_slots, slots.at[me], slot_send.at[d], slot_recv.at[d], (peer, z))

    def decay_copy(d, peer):
        return remote(own_decay, decays.at[me], decay_send.at[d], decay_recv.at[d], (peer, z))

    def cache_copy(d, peer):
        return remote(strip(cache, peer), part(pieces, me), cache_send.at[d], cache_recv.at[d], (peer, z))

    def kv_copy(d, peer):
        return remote(strip(kv, peer), part(kv_pieces, me), kv_send.at[d], kv_recv.at[d], (peer, z))

    def hit_copy(d, peer):
        return remote(part(hit_pieces, peer), strip(prefix, me), hit_send.at[d], hit_recv.at[d], (peer, z))

    def new_copy(d, peer):
        return remote(part(new_pieces, peer), strip(new_cache, me), new_send.at[d], new_recv.at[d], (peer, z))

    def square_copy(d, peer):
        return remote(own_squares, squares.at[z], square_send.at[d], square_recv.at[d], (me, peer))

    barrier = pltpu.get_barrier_semaphore()
    each_peer(lambda d, p: pl.semaphore_signal(barrier, inc=1, device_id=(p, z), device_id_type=MESH))
    each_z(lambda d, p: pl.semaphore_signal(barrier, inc=1, device_id=(me, p), device_id_type=MESH))

    own_cache_copy = pltpu.make_async_copy(strip(cache, me), part(pieces, me), local_sem.at[0])
    own_cache_copy.start()
    none = pieces.shape[0] - 8
    pieces[pl.ds(none, 8)] = jnp.zeros((8, rows, LANES), F32)
    lane = lax.broadcasted_iota(jnp.int32, (1, LANES), 1)
    table = jnp.zeros((1, LANES), jnp.int32)
    for r in range(count):
        hit, write = hit_entry[r], write_entry[r]
        hit_slot = jnp.where(hit >= 0, entry_slot[jnp.maximum(hit, 0)], none)
        write_slot = jnp.where(write >= 0, entry_slot[jnp.maximum(write, 0)], -1)
        table = jnp.where(lane == HIT + r, hit_slot, table)
        table = jnp.where(lane == WRITE + r, write_slot, table)
    own_slots[...] = table
    slots[me] = table
    pl.semaphore_wait(barrier, n - 1 + nz - 1)

    each_peer(lambda d, p: slot_copy(d, p).start())
    each_peer(lambda d, p: cache_copy(d, p).start())

    low = lax.broadcasted_iota(jnp.int32, (length, length), 0)
    col = lax.broadcasted_iota(jnp.int32, (length, length), 1)
    causal = low >= col
    lower, upper = jnp.where(causal, 1.0, 0.0), jnp.where(low <= col, 1.0, 0.0)

    def block(r, decay_row):
        steps = log_decay[r]
        high = dict(precision=lax.Precision.HIGHEST)
        gsum_rows = jnp.dot(steps, upper, preferred_element_type=F32, **high)
        gsum_cols = nt(lower, steps, **high)
        last = gsum_rows[:, length - 1 : length]
        grown = jnp.exp(gsum_cols)
        for h in range(head_count):
            cols = slice(h * size, (h + 1) * size)
            q, k, v = queries[r, :, cols], key_rows[r, :, cols], values[r, :, cols]
            gcol, grow, glast = gsum_cols[:, h : h + 1], gsum_rows[h : h + 1], last[h : h + 1]
            gap = jnp.where(causal, jnp.exp(jnp.minimum(gcol - grow, 0.0)), 0.0)
            weights = (nt(q, k) * gap).astype(BF16)
            heads[r, :, cols] = jnp.dot(weights, v, preferred_element_type=F32)
            weighted = (k.astype(F32) * jnp.exp(glast - gcol)).astype(BF16)
            kv[r, h * size : (h + 1) * size, :] = tn(weighted, v)
            decay_cols[r, :, cols] = jnp.broadcast_to(grown[:, h : h + 1], (length, size))
            decay_row = jnp.where(lane == r * head_count + h, jnp.exp(glast), decay_row)
        return decay_row

    decay_row = lax.fori_loop(0, count, block, jnp.zeros((1, LANES), F32))
    own_decay[...] = decay_row
    decays[me] = decay_row
    own_kv_copy = pltpu.make_async_copy(strip(kv, me), part(kv_pieces, me), local_sem.at[1])
    own_kv_copy.start()
    each_peer(lambda d, p: decay_copy(d, p).start())
    each_peer(lambda d, p: kv_copy(d, p).start())

    each_peer(lambda d, p: slot_copy(d, p).wait_recv())
    to_scalar = pltpu.make_async_copy(slots, slots_s, local_sem.at[2])
    to_scalar.start()
    to_scalar.wait()
    place = (
        lax.broadcasted_iota(jnp.int32, (8, LANES), 0) * LANES
        + lax.broadcasted_iota(jnp.int32, (8, LANES), 1)
    )

    def invert(device, found):
        for r in range(count):
            found = jnp.where(place == slots_s[device, 0, WRITE + r], device * 16 + r + 1, found)
        return found

    inverse[...] = lax.fori_loop(0, n, invert, jnp.zeros((8, LANES), jnp.int32))
    to_scalar = pltpu.make_async_copy(inverse, inverse_s, local_sem.at[3])
    to_scalar.start()
    to_scalar.wait()

    own_cache_copy.wait()
    each_peer(lambda d, p: cache_copy(d, p).wait_recv())

    def pick(device, carry):
        for r in range(count):
            hit_pieces[device * count + r] = pieces[slots_s[device, 0, HIT + r]]
        return carry

    lax.fori_loop(0, n, pick, 0)
    own_hit_copy = pltpu.make_async_copy(part(hit_pieces, me), strip(prefix, me), local_sem.at[4])
    own_hit_copy.start()
    each_peer(lambda d, p: hit_copy(d, p).start())

    each_peer(lambda d, p: decay_copy(d, p).wait_recv())
    to_scalar = pltpu.make_async_copy(decays, decays_s, local_sem.at[5])
    to_scalar.start()
    to_scalar.wait()
    own_kv_copy.wait()
    each_peer(lambda d, p: kv_copy(d, p).wait_recv())
    my_head = (me * rows) // size

    def renew(device, carry):
        for e in range(count):
            slot = device * count + e
            code = inverse_s[slot // LANES, slot % LANES]
            writer = jnp.maximum(code - 1, 0)
            source, r = writer // 16, writer % 16
            state = decays_s[source, 0, r * head_count + my_head] * pieces[slots_s[source, 0, HIT + r]]
            state = state + kv_pieces[source * count + r]
            new_pieces[slot] = jnp.where(code > 0, state, pieces[slot])
        return carry

    lax.fori_loop(0, n, renew, 0)
    own_new_copy = pltpu.make_async_copy(part(new_pieces, me), strip(new_cache, me), local_sem.at[6])
    own_new_copy.start()
    each_peer(lambda d, p: new_copy(d, p).start())

    own_hit_copy.wait()
    each_peer(lambda d, p: hit_copy(d, p).wait_recv())
    lane_wide = lax.broadcasted_iota(jnp.int32, (length, LANES), 1)

    def carry_in(r, sums):
        total = jnp.zeros((length, 1), F32)
        for h in range(head_count):
            cols = slice(h * size, (h + 1) * size)
            state = prefix[r, h * size : (h + 1) * size, :]
            state_high = state.astype(BF16)
            state_low = (state - state_high.astype(F32)).astype(BF16)
            q = queries[r, :, cols]
            carried = jnp.dot(q, state_high, preferred_element_type=F32)
            carried = carried + jnp.dot(q, state_low, preferred_element_type=F32)
            out = heads[r, :, cols] + carried * decay_cols[r, :, cols]
            heads[r, :, cols] = out
            total = total + jnp.sum(out * out, axis=1, keepdims=True)
        return jnp.where(lane_wide == r, total, sums)

    sums = lax.fori_loop(0, count, carry_in, jnp.zeros((length, LANES), F32))
    flat = jnp.transpose(sums)
    packed = jnp.concatenate([flat[0:8], flat[8:16]], axis=1)
    own_squares[...] = packed
    squares[z] = packed
    each_z(lambda d, p: square_copy(d, p).start())
    each_z(lambda d, p: square_copy(d, p).wait_recv())
    total = jnp.sum(squares[...], axis=0)
    inv = lax.rsqrt(total / (width * nz) + 1e-06)
    inv = jnp.transpose(inv)

    def norm(r, carry):
        low_half = jnp.sum(jnp.where(lane8 == r, inv[0:length], 0.0), axis=1, keepdims=True)
        high_half = jnp.sum(jnp.where(lane8 == r - 8, inv[length:], 0.0), axis=1, keepdims=True)
        scale = low_half + high_half
        attended[r] = (heads[r] * scale * gain[...]).astype(BF16)
        return carry

    lane8 = lax.broadcasted_iota(jnp.int32, (length, 8), 1)
    lax.fori_loop(0, count, norm, 0)

    own_new_copy.wait()
    each_peer(lambda d, p: new_copy(d, p).wait_recv())
    each_peer(lambda d, p: slot_copy(d, p).wait_send())
    each_peer(lambda d, p: decay_copy(d, p).wait_send())
    each_peer(lambda d, p: cache_copy(d, p).wait_send())
    each_peer(lambda d, p: kv_copy(d, p).wait_send())
    each_peer(lambda d, p: hit_copy(d, p).wait_send())
    each_peer(lambda d, p: new_copy(d, p).wait_send())
    each_z(lambda d, p: square_copy(d, p).wait_send())


def body(
    n, nz, queries, key_rows, values, log_decay, state_cache, norm_gain, entry_slot, hit_entry, write_entry
):
    count, length, width = queries.shape
    entries, head_count, size, _ = state_cache.shape
    tall = head_count * size
    rows = tall // n
    vmem, smem = pl.BlockSpec(memory_space=pltpu.VMEM), pl.BlockSpec(memory_space=pltpu.SMEM)
    anywhere = pl.BlockSpec(memory_space=pl.ANY)
    sem = pltpu.SemaphoreType.DMA
    attended, new_cache = pl.pallas_call(
        functools.partial(kernel, n, nz),
        out_shape=(
            jax.ShapeDtypeStruct((count, length, width), BF16),
            jax.ShapeDtypeStruct((entries, tall, size), F32),
        ),
        in_specs=[smem, smem, smem, vmem, vmem, vmem, vmem, vmem, anywhere],
        out_specs=(vmem, anywhere),
        scratch_shapes=[
            pltpu.VMEM((n * entries + 8, rows, size), F32),
            pltpu.VMEM((n * count, rows, size), F32),
            pltpu.VMEM((count, tall, size), F32),
            pltpu.VMEM((n * count, rows, size), F32),
            pltpu.VMEM((n * entries, rows, size), F32),
            pltpu.VMEM((count, tall, size), F32),
            pltpu.VMEM((count, length, width), F32),
            pltpu.VMEM((count, length, width), F32),
            pltpu.VMEM((1, LANES), jnp.int32),
            pltpu.VMEM((n, 1, LANES), jnp.int32),
            pltpu.VMEM((1, LANES), F32),
            pltpu.VMEM((n, 1, LANES), F32),
            pltpu.VMEM((8, LANES), jnp.int32),
            pltpu.VMEM((8, LANES), F32),
            pltpu.VMEM((nz, 8, LANES), F32),
            pltpu.SMEM((n, 1, LANES), jnp.int32),
            pltpu.SMEM((n, 1, LANES), F32),
            pltpu.SMEM((8, LANES), jnp.int32),
            *[sem((n,))] * 12,
            sem((nz,)),
            sem((nz,)),
            sem((7,)),
        ],
        compiler_params=pltpu.CompilerParams(
            collective_id=0, has_side_effects=True, vmem_limit_bytes=32 << 20
        ),
    )(
        entry_slot, hit_entry, write_entry, log_decay, queries, key_rows, values,
        norm_gain.reshape(1, width), state_cache.reshape(entries, tall, size),
    )
    return attended, new_cache.reshape(state_cache.shape)


def solution(mesh):
    placed = (
        P("req", None, "head"),
        P("req", None, "head"),
        P("req", None, "head"),
        P("req", "head", None),
        P("req", "head", None, None),
        P("head"),
        P(),
        P("req"),
        P("req"),
    )
    return jax.shard_map(
        functools.partial(body, mesh.shape["req"], mesh.shape["head"]),
        mesh=mesh,
        in_specs=placed,
        out_specs=(P("req", None, "head"), P("req", "head", None, None)),
        check_vma=False,
    )
```

```python
import functools

import jax
import jax.numpy as jnp
from jax import lax
from jax.experimental import pallas as pl
from jax.experimental.pallas import tpu as pltpu
from jax.sharding import PartitionSpec as P

MESH = pl.DeviceIdType.MESH
F32 = jnp.float32
BF16 = jnp.bfloat16
LANES = 128
HIT, WRITE = 0, 16
STRIDE = 5


def nt(a, b, **kw):
    return lax.dot_general(a, b, (((1,), (1,)), ((), ())), preferred_element_type=F32, **kw)


def tn(a, b):
    return lax.dot_general(a, b, (((0,), (0,)), ((), ())), preferred_element_type=F32)


def kernel(
    n, nz, slot_hbm, hit_hbm, write_hbm, log_decay_hbm, queries_hbm, key_rows_hbm, values_hbm, gain_hbm, cache,
    attended, new_cache,
    pieces, kv_pieces, kv, hit_pieces, new_pieces, prefix, heads, decay_cols, own_slots, slots,
    own_decay, decays, source_rows, source_decay, own_squares, squares, log_decay, queries, key_rows, values, gain,
    slots_s, decays_s, source_rows_s, source_decay_s, entry_slot, hit_entry, write_entry,
    slot_send, slot_recv, decay_send, decay_recv, cache_send, cache_recv, kv_send, kv_recv,
    hit_send, hit_recv, new_send, new_recv, square_send, square_recv, local_sem, plane_in, planes_in,
):
    count, length, width = queries.shape
    head_count = log_decay.shape[1]
    size = width // head_count
    rows = cache.shape[1] // n
    me, z = lax.axis_index("req"), lax.axis_index("head")

    def peer_of(d):
        x, y, c = me // 8, (me // 2) % 4, me % 2
        return ((x + d // 8) % 4) * 8 + ((y + (d // 2) % 4) % 4) * 2 + (c + d % 2) % 2

    def each_peer(act, low=1, high=n):
        def step(i, carry):
            d = (i * STRIDE) % n
            act(d, peer_of(d))
            return carry

        lax.fori_loop(low, high, step, 0)

    def each_z(act):
        def step(d, carry):
            act(d, lax.rem(z + d, nz))
            return carry

        lax.fori_loop(1, nz, step, 0)

    def remote(src, dst, send, recv, device):
        return pltpu.make_async_remote_copy(
            src_ref=src, dst_ref=dst, send_sem=send, recv_sem=recv, device_id=device, device_id_type=MESH
        )

    def part(ref, device):
        return ref.at[pl.ds(device * count, count)]

    def strip(ref, device):
        return ref.at[:, pl.ds(pl.multiple_of(device * rows, rows), rows), :]

    def slot_copy(d, peer):
        return remote(own_slots, slots.at[me], slot_send.at[d], slot_recv.at[d], (peer, z))

    def decay_copy(d, peer):
        return remote(own_decay, decays.at[me], decay_send.at[d], decay_recv.at[d], (peer, z))

    def cache_copy(d, peer):
        return remote(strip(cache, peer), part(pieces, me), cache_send.at[d], cache_recv.at[d], (peer, z))

    def kv_copy(d, peer):
        return remote(strip(kv, peer), part(kv_pieces, me), kv_send.at[d], kv_recv.at[d], (peer, z))

    def hit_copy(d, peer):
        return remote(part(hit_pieces, peer), strip(prefix, me), hit_send.at[d], hit_recv.at[d], (peer, z))

    def new_copy(d, peer):
        return remote(part(new_pieces, peer), strip(new_cache, me), new_send.at[d], new_recv.at[d], (peer, z))

    def square_copy(d, peer):
        return remote(own_squares, squares.at[z], square_send.at[d], square_recv.at[d], (me, peer))

    barrier = pltpu.get_barrier_semaphore()
    last = n - 1

    def signal(semaphore, device):
        pl.semaphore_signal(semaphore, inc=1, device_id=device, device_id_type=MESH)

    def greet(d, p):
        @pl.when(p != last)
        def _():
            signal(barrier, (p, z))

    each_peer(greet)

    def fetch(src, dst, k):
        copy = pltpu.make_async_copy(src, dst, local_sem.at[k])
        copy.start()
        return copy

    tables_in = [
        fetch(hit_hbm, hit_entry, 0),
        fetch(write_hbm, write_entry, 1),
        fetch(slot_hbm, entry_slot, 2),
        fetch(log_decay_hbm, log_decay, 3),
    ]
    rows_in = [
        fetch(queries_hbm, queries, 4),
        fetch(key_rows_hbm, key_rows, 5),
        fetch(values_hbm, values, 6),
        fetch(gain_hbm, gain, 7),
    ]
    own_cache_copy = fetch(strip(cache, me), part(pieces, me), 8)
    none = n * count
    pieces[pl.ds(none, 8)] = jnp.zeros((8, rows, LANES), F32)
    kv_pieces[pl.ds(none, 8)] = jnp.zeros((8, rows, LANES), F32)

    @pl.when(me != last)
    def _():
        pl.semaphore_wait(barrier, n - 1)

    @pl.when(me == last - 1)
    def _():
        signal(plane_in, (last, z))

    @pl.when(me == last)
    def _():
        pl.semaphore_wait(plane_in, 1)
        each_z(lambda d, p: signal(barrier, (me, p)))

    each_peer(lambda d, p: cache_copy(d, p).start(), 1, n // 4)
    for copy in tables_in:
        copy.wait()
    lane = lax.broadcasted_iota(jnp.int32, (1, LANES), 1)
    table = jnp.zeros((1, LANES), jnp.int32)
    decay_row = jnp.zeros((1, LANES), F32)
    for r in range(count):
        hit, write = hit_entry[r], write_entry[r]
        hit_slot = jnp.where(hit >= 0, entry_slot[jnp.maximum(hit, 0)], none)
        write_slot = jnp.where(write >= 0, entry_slot[jnp.maximum(write, 0)], -1)
        table = jnp.where(lane == HIT + r, hit_slot, table)
        table = jnp.where(lane == WRITE + r, write_slot, table)
        whole = jnp.exp(jnp.sum(log_decay[r], axis=1, keepdims=True))
        for h in range(head_count):
            decay_row = jnp.where(lane == r * head_count + h, whole[h : h + 1], decay_row)
    own_slots[...] = table
    slots[me] = table
    own_decay[...] = decay_row
    decays[me] = decay_row
    each_peer(lambda d, p: slot_copy(d, p).start())
    each_peer(lambda d, p: decay_copy(d, p).start())
    each_peer(lambda d, p: cache_copy(d, p).start(), n // 4, n)
    for copy in rows_in:
        copy.wait()

    low = lax.broadcasted_iota(jnp.int32, (length, length), 0)
    col = lax.broadcasted_iota(jnp.int32, (length, length), 1)
    causal = low >= col
    lower, upper = jnp.where(causal, 1.0, 0.0), jnp.where(low <= col, 1.0, 0.0)

    def block(r, carry):
        steps = log_decay[r]
        high = dict(precision=lax.Precision.HIGHEST)
        gsum_rows = jnp.dot(steps, upper, preferred_element_type=F32, **high)
        gsum_cols = nt(lower, steps, **high)
        last = gsum_rows[:, length - 1 : length]
        grown = jnp.exp(gsum_cols)
        for h in range(head_count):
            cols = slice(h * size, (h + 1) * size)
            q, k, v = queries[r, :, cols], key_rows[r, :, cols], values[r, :, cols]
            gcol, grow, glast = gsum_cols[:, h : h + 1], gsum_rows[h : h + 1], last[h : h + 1]
            gap = jnp.where(causal, jnp.exp(jnp.minimum(gcol - grow, 0.0)), 0.0)
            weights = (nt(q, k) * gap).astype(BF16)
            heads[r, :, cols] = jnp.dot(weights, v, preferred_element_type=F32)
            weighted = (k.astype(F32) * jnp.exp(glast - gcol)).astype(BF16)
            kv[r, h * size : (h + 1) * size, :] = tn(weighted, v)
            decay_cols[r, :, cols] = jnp.broadcast_to(grown[:, h : h + 1], (length, size))
        return carry

    lax.fori_loop(0, count, block, 0)

    each_peer(lambda d, p: slot_copy(d, p).wait_recv())
    each_peer(lambda d, p: decay_copy(d, p).wait_recv())
    for copy in [fetch(slots, slots_s, 9), fetch(decays, decays_s, 10)]:
        copy.wait()
    place = (
        lax.broadcasted_iota(jnp.int32, (8, LANES), 0) * LANES
        + lax.broadcasted_iota(jnp.int32, (8, LANES), 1)
    )
    my_head = (me * rows) // size

    def invert(device, found):
        hit_row, kv_row, decay = found
        for r in range(count):
            here = place == slots_s[device, 0, WRITE + r]
            hit_row = jnp.where(here, slots_s[device, 0, HIT + r], hit_row)
            kv_row = jnp.where(here, device * count + r, kv_row)
            decay = jnp.where(here, decays_s[device, 0, r * head_count + my_head], decay)
        return hit_row, kv_row, decay

    hit_row, kv_row, decay = lax.fori_loop(
        0, n, invert, (place, jnp.full((8, LANES), none, jnp.int32), jnp.ones((8, LANES), F32))
    )
    source_rows[0] = hit_row
    source_rows[1] = kv_row
    source_decay[...] = decay
    sources_in = [fetch(source_rows, source_rows_s, 11), fetch(source_decay, source_decay_s, 12)]

    own_kv_copy = fetch(strip(kv, me), part(kv_pieces, me), 13)

    def send_kv(d, p):
        cache_copy(d, p).wait_send()
        kv_copy(d, p).start()

    each_peer(send_kv)

    own_cache_copy.wait()
    each_peer(lambda d, p: cache_copy(d, p).wait_recv())

    def pick(device):
        for r in range(count):
            hit_pieces[device * count + r] = pieces[slots_s[device, 0, HIT + r]]

    def send_hits(d, p):
        pick(p)
        kv_copy(d, p).wait_send()
        hit_copy(d, p).start()

    each_peer(send_hits)
    pick(me)
    own_hit_copy = fetch(part(hit_pieces, me), strip(prefix, me), 14)

    @pl.when(me == last)
    def _():
        pl.semaphore_wait(barrier, nz - 1)
        each_peer(lambda d, p: signal(planes_in, (p, z)))

    own_kv_copy.wait()
    each_peer(lambda d, p: kv_copy(d, p).wait_recv())
    for copy in sources_in:
        copy.wait()

    def renew(device):
        for e in range(count):
            slot = device * count + e
            sub, at = slot // LANES, slot % LANES
            state = source_decay_s[sub, at] * pieces[source_rows_s[0, sub, at]]
            new_pieces[slot] = state + kv_pieces[source_rows_s[1, sub, at]]

    def send_new(d, p):
        renew(p)
        hit_copy(d, p).wait_send()
        new_copy(d, p).start()

    each_peer(send_new)
    renew(me)
    own_new_copy = fetch(part(new_pieces, me), strip(new_cache, me), 15)

    own_hit_copy.wait()
    each_peer(lambda d, p: hit_copy(d, p).wait_recv())
    lane_wide = lax.broadcasted_iota(jnp.int32, (length, LANES), 1)

    def carry_in(r, sums):
        total = jnp.zeros((length, 1), F32)
        for h in range(head_count):
            cols = slice(h * size, (h + 1) * size)
            state = prefix[r, h * size : (h + 1) * size, :]
            state_high = state.astype(BF16)
            state_low = (state - state_high.astype(F32)).astype(BF16)
            q = queries[r, :, cols]
            carried = jnp.dot(q, state_high, preferred_element_type=F32)
            carried = carried + jnp.dot(q, state_low, preferred_element_type=F32)
            out = heads[r, :, cols] + carried * decay_cols[r, :, cols]
            heads[r, :, cols] = out
            total = total + jnp.sum(out * out, axis=1, keepdims=True)
        return jnp.where(lane_wide == r, total, sums)

    sums = lax.fori_loop(0, count, carry_in, jnp.zeros((length, LANES), F32))
    flat = jnp.transpose(sums)
    packed = jnp.concatenate([flat[0:8], flat[8:16]], axis=1)
    own_squares[...] = packed
    squares[z] = packed

    @pl.when(me != last)
    def _():
        pl.semaphore_wait(planes_in, 1)

    each_z(lambda d, p: square_copy(d, p).start())
    each_z(lambda d, p: square_copy(d, p).wait_recv())
    total = jnp.sum(squares[...], axis=0)
    inv = lax.rsqrt(total / (width * nz) + 1e-06)
    inv = jnp.transpose(inv)

    def norm(r, carry):
        low_half = jnp.sum(jnp.where(lane8 == r, inv[0:length], 0.0), axis=1, keepdims=True)
        high_half = jnp.sum(jnp.where(lane8 == r - 8, inv[length:], 0.0), axis=1, keepdims=True)
        scale = low_half + high_half
        attended[r] = (heads[r] * scale * gain[...]).astype(BF16)
        return carry

    lane8 = lax.broadcasted_iota(jnp.int32, (length, 8), 1)
    lax.fori_loop(0, count, norm, 0)

    own_new_copy.wait()
    each_peer(lambda d, p: new_copy(d, p).wait_recv())
    each_peer(lambda d, p: slot_copy(d, p).wait_send())
    each_peer(lambda d, p: decay_copy(d, p).wait_send())
    each_peer(lambda d, p: new_copy(d, p).wait_send())
    each_z(lambda d, p: square_copy(d, p).wait_send())


def body(
    n, nz, queries, key_rows, values, log_decay, state_cache, norm_gain, entry_slot, hit_entry, write_entry
):
    count, length, width = queries.shape
    entries, head_count, size, _ = state_cache.shape
    tall = head_count * size
    rows = tall // n
    vmem, hbm = pl.BlockSpec(memory_space=pltpu.VMEM), pl.BlockSpec(memory_space=pltpu.HBM)
    sem = pltpu.SemaphoreType.DMA
    attended, new_cache = pl.pallas_call(
        functools.partial(kernel, n, nz),
        out_shape=(
            pltpu.VMEM((count, length, width), BF16),
            pltpu.VMEM((entries, tall, size), F32),
        ),
        in_specs=[hbm] * 9,
        out_specs=(vmem, vmem),
        scratch_shapes=[
            pltpu.VMEM((n * entries + 8, rows, size), F32),
            pltpu.VMEM((n * count + 8, rows, size), F32),
            pltpu.VMEM((count, tall, size), F32),
            pltpu.VMEM((n * count, rows, size), F32),
            pltpu.VMEM((n * entries, rows, size), F32),
            pltpu.VMEM((count, tall, size), F32),
            pltpu.VMEM((count, length, width), F32),
            pltpu.VMEM((count, length, width), F32),
            pltpu.VMEM((1, LANES), jnp.int32),
            pltpu.VMEM((n, 1, LANES), jnp.int32),
            pltpu.VMEM((1, LANES), F32),
            pltpu.VMEM((n, 1, LANES), F32),
            pltpu.VMEM((2, 8, LANES), jnp.int32),
            pltpu.VMEM((8, LANES), F32),
            pltpu.VMEM((8, LANES), F32),
            pltpu.VMEM((nz, 8, LANES), F32),
            pltpu.VMEM(log_decay.shape, F32),
            *[pltpu.VMEM((count, length, width), BF16)] * 3,
            pltpu.VMEM((1, width), F32),
            pltpu.SMEM((n, 1, LANES), jnp.int32),
            pltpu.SMEM((n, 1, LANES), F32),
            pltpu.SMEM((2, 8, LANES), jnp.int32),
            pltpu.SMEM((8, LANES), F32),
            pltpu.SMEM(entry_slot.shape, jnp.int32),
            pltpu.SMEM(hit_entry.shape, jnp.int32),
            pltpu.SMEM(write_entry.shape, jnp.int32),
            *[sem((n,))] * 12,
            sem((nz,)),
            sem((nz,)),
            sem((16,)),
            pltpu.SemaphoreType.REGULAR,
            pltpu.SemaphoreType.REGULAR,
        ],
        compiler_params=pltpu.CompilerParams(
            collective_id=0, has_side_effects=True, vmem_limit_bytes=32 << 20
        ),
    )(
        *(
            pltpu.with_memory_space_constraint(x, pltpu.HBM)
            for x in (
                entry_slot, hit_entry, write_entry, log_decay, queries, key_rows, values,
                norm_gain.reshape(1, width), state_cache.reshape(entries, tall, size),
            )
        )
    )
    return attended, new_cache.reshape(state_cache.shape)


def solution(mesh):
    placed = (
        P("req", None, "head"),
        P("req", None, "head"),
        P("req", None, "head"),
        P("req", "head", None),
        P("req", "head", None, None),
        P("head"),
        P(),
        P("req"),
        P("req"),
    )
    return jax.shard_map(
        functools.partial(body, mesh.shape["req"], mesh.shape["head"]),
        mesh=mesh,
        in_specs=placed,
        out_specs=(P("req", None, "head"), P("req", "head", None, None)),
        check_vma=False,
    )
```

```python
import functools

import jax
import jax.numpy as jnp
from jax import lax
from jax.experimental import pallas as pl
from jax.experimental.pallas import tpu as pltpu
from jax.sharding import PartitionSpec as P

MESH = pl.DeviceIdType.MESH
F32 = jnp.float32
BF16 = jnp.bfloat16
LANES = 128
HIT, WRITE = 0, 16
STRIDE = 5


def nt(a, b, **kw):
    return lax.dot_general(a, b, (((1,), (1,)), ((), ())), preferred_element_type=F32, **kw)


def tn(a, b):
    return lax.dot_general(a, b, (((0,), (0,)), ((), ())), preferred_element_type=F32)


def kernel(
    n, nz, slot_hbm, hit_hbm, write_hbm, log_decay_hbm, queries_hbm, key_rows_hbm, values_hbm, gain_hbm, cache,
    attended, new_cache,
    pieces, kv_pieces, kv, hit_pieces, new_pieces, prefix, heads, decay_cols, own_slots, slots,
    own_decay, decays, source_rows, source_decay, own_squares, squares, log_decay, queries, key_rows, values, gain,
    slots_s, decays_s, source_rows_s, source_decay_s, entry_slot, hit_entry, write_entry,
    slot_send, slot_recv, decay_send, decay_recv, cache_send, cache_recv, kv_send, kv_recv,
    hit_send, hit_recv, new_send, new_recv, square_send, square_recv, local_sem, plane_in, planes_in,
):
    count, length, width = queries.shape
    head_count = log_decay.shape[1]
    size = width // head_count
    rows = cache.shape[1] // n
    me, z = lax.axis_index("req"), lax.axis_index("head")

    core = lax.rem(me, 2)
    y2 = lax.rem(me, 8) - core
    x8 = me - lax.rem(me, 8)

    def each_peer(act, low=1, high=n):
        def step(i, carry):
            d = lax.rem(i * STRIDE, n)
            within = lax.rem(d, 8)
            side = lax.rem(d, 2)
            act(lax.rem(x8 + d - within, n) + lax.rem(y2 + within - side, 8) + lax.rem(core + side, 2))
            return carry

        lax.fori_loop(low, high, step, 0)

    def each_z(act):
        def step(d, carry):
            act(lax.rem(z + d, nz))
            return carry

        lax.fori_loop(1, nz, step, 0)

    def remote(src, dst, send, recv, device):
        return pltpu.make_async_remote_copy(
            src_ref=src, dst_ref=dst, send_sem=send, recv_sem=recv, device_id=device, device_id_type=MESH
        )

    def part(ref, device):
        return ref.at[pl.ds(device * count, count)]

    def strip(ref, device):
        return ref.at[:, pl.ds(pl.multiple_of(device * rows, rows), rows), :]

    def slot_copy(peer):
        return remote(own_slots, slots.at[me], slot_send, slot_recv, (peer, z))

    def decay_copy(peer):
        return remote(own_decay, decays.at[me], decay_send, decay_recv, (peer, z))

    def cache_copy(peer):
        return remote(strip(cache, peer), part(pieces, me), cache_send, cache_recv, (peer, z))

    def kv_copy(peer):
        return remote(strip(kv, peer), part(kv_pieces, me), kv_send, kv_recv, (peer, z))

    def hit_copy(peer):
        return remote(part(hit_pieces, peer), strip(prefix, me), hit_send, hit_recv, (peer, z))

    def new_copy(peer):
        return remote(part(new_pieces, peer), strip(new_cache, me), new_send, new_recv, (peer, z))

    def square_copy(peer):
        return remote(own_squares, squares.at[z], square_send, square_recv, (me, peer))

    def await_all(ref, semaphore, amount):
        whole = ref.at[pl.ds(0, amount)]
        pltpu.make_async_copy(whole, whole, semaphore).wait()

    others, other_pieces = n - 1, (n - 1) * count

    barrier = pltpu.get_barrier_semaphore()
    last = n - 1

    def signal(semaphore, device):
        pl.semaphore_signal(semaphore, inc=1, device_id=device, device_id_type=MESH)

    def greet(p):
        @pl.when(p != last)
        def _():
            signal(barrier, (p, z))

    each_peer(greet)

    def fetch(src, dst, k):
        copy = pltpu.make_async_copy(src, dst, local_sem.at[k])
        copy.start()
        return copy

    tables_in = [
        fetch(hit_hbm, hit_entry, 0),
        fetch(write_hbm, write_entry, 1),
        fetch(slot_hbm, entry_slot, 2),
        fetch(log_decay_hbm, log_decay, 3),
    ]
    rows_in = [
        fetch(queries_hbm, queries, 4),
        fetch(key_rows_hbm, key_rows, 5),
        fetch(values_hbm, values, 6),
        fetch(gain_hbm, gain, 7),
    ]
    own_cache_copy = fetch(strip(cache, me), part(pieces, me), 8)
    none = n * count
    pieces[pl.ds(none, 8)] = jnp.zeros((8, rows, LANES), F32)
    kv_pieces[pl.ds(none, 8)] = jnp.zeros((8, rows, LANES), F32)

    @pl.when(me != last)
    def _():
        pl.semaphore_wait(barrier, n - 1)

    @pl.when(me == last - 1)
    def _():
        signal(plane_in, (last, z))

    @pl.when(me == last)
    def _():
        pl.semaphore_wait(plane_in, 1)
        each_z(lambda p: signal(barrier, (me, p)))

    each_peer(lambda p: cache_copy(p).start(), 1, n // 4)
    for copy in tables_in:
        copy.wait()
    lane = lax.broadcasted_iota(jnp.int32, (1, LANES), 1)
    table = jnp.zeros((1, LANES), jnp.int32)
    decay_row = jnp.zeros((1, LANES), F32)
    for r in range(count):
        hit, write = hit_entry[r], write_entry[r]
        hit_slot = jnp.where(hit >= 0, entry_slot[jnp.maximum(hit, 0)], none)
        write_slot = jnp.where(write >= 0, entry_slot[jnp.maximum(write, 0)], -1)
        table = jnp.where(lane == HIT + r, hit_slot, table)
        table = jnp.where(lane == WRITE + r, write_slot, table)
        whole = jnp.exp(jnp.sum(log_decay[r], axis=1, keepdims=True))
        for h in range(head_count):
            decay_row = jnp.where(lane == r * head_count + h, whole[h : h + 1], decay_row)
    own_slots[...] = table
    slots[me] = table
    own_decay[...] = decay_row
    decays[me] = decay_row
    each_peer(lambda p: slot_copy(p).start())
    each_peer(lambda p: decay_copy(p).start())
    each_peer(lambda p: cache_copy(p).start(), n // 4, n)
    for copy in rows_in:
        copy.wait()

    low = lax.broadcasted_iota(jnp.int32, (length, length), 0)
    col = lax.broadcasted_iota(jnp.int32, (length, length), 1)
    causal = low >= col
    lower, upper = jnp.where(causal, 1.0, 0.0), jnp.where(low <= col, 1.0, 0.0)

    def block(r, carry):
        steps = log_decay[r]
        high = dict(precision=lax.Precision.HIGHEST)
        gsum_rows = jnp.dot(steps, upper, preferred_element_type=F32, **high)
        gsum_cols = nt(lower, steps, **high)
        last = gsum_rows[:, length - 1 : length]
        grown = jnp.exp(gsum_cols)
        for h in range(head_count):
            cols = slice(h * size, (h + 1) * size)
            q, k, v = queries[r, :, cols], key_rows[r, :, cols], values[r, :, cols]
            gcol, grow, glast = gsum_cols[:, h : h + 1], gsum_rows[h : h + 1], last[h : h + 1]
            gap = jnp.where(causal, jnp.exp(jnp.minimum(gcol - grow, 0.0)), 0.0)
            weights = (nt(q, k) * gap).astype(BF16)
            heads[r, :, cols] = jnp.dot(weights, v, preferred_element_type=F32)
            weighted = (k.astype(F32) * jnp.exp(glast - gcol)).astype(BF16)
            kv[r, h * size : (h + 1) * size, :] = tn(weighted, v)
            decay_cols[r, :, cols] = jnp.broadcast_to(grown[:, h : h + 1], (length, size))
        return carry

    lax.fori_loop(0, count, block, 0)
    own_kv_copy = fetch(strip(kv, me), part(kv_pieces, me), 13)

    each_peer(lambda p: kv_copy(p).start())

    await_all(slots, slot_recv, others)
    await_all(decays, decay_recv, others)
    for copy in [fetch(slots, slots_s, 9), fetch(decays, decays_s, 10)]:
        copy.wait()
    place = (
        lax.broadcasted_iota(jnp.int32, (8, LANES), 0) * LANES
        + lax.broadcasted_iota(jnp.int32, (8, LANES), 1)
    )
    my_head = (me * rows) // size

    def invert(device, found):
        hit_row, kv_row, decay = found
        for r in range(count):
            here = place == slots_s[device, 0, WRITE + r]
            hit_row = jnp.where(here, slots_s[device, 0, HIT + r], hit_row)
            kv_row = jnp.where(here, device * count + r, kv_row)
            decay = jnp.where(here, decays_s[device, 0, r * head_count + my_head], decay)
        return hit_row, kv_row, decay

    hit_row, kv_row, decay = lax.fori_loop(
        0, n, invert, (place, jnp.full((8, LANES), none, jnp.int32), jnp.ones((8, LANES), F32))
    )
    source_rows[0] = hit_row
    source_rows[1] = kv_row
    source_decay[...] = decay
    sources_in = [fetch(source_rows, source_rows_s, 11), fetch(source_decay, source_decay_s, 12)]


    own_cache_copy.wait()
    await_all(pieces, cache_recv, other_pieces)

    def pick(device):
        for r in range(count):
            hit_pieces[device * count + r] = pieces[slots_s[device, 0, HIT + r]]

    def send_hits(p):
        pick(p)
        hit_copy(p).start()

    each_peer(send_hits)
    pick(me)
    own_hit_copy = fetch(part(hit_pieces, me), strip(prefix, me), 14)

    @pl.when(me == last)
    def _():
        pl.semaphore_wait(barrier, nz - 1)
        each_peer(lambda p: signal(planes_in, (p, z)))

    own_kv_copy.wait()
    await_all(kv_pieces, kv_recv, other_pieces)
    for copy in sources_in:
        copy.wait()

    def renew(device):
        for e in range(count):
            slot = device * count + e
            sub, at = lax.div(slot, LANES), lax.rem(slot, LANES)
            state = source_decay_s[sub, at] * pieces[source_rows_s[0, sub, at]]
            new_pieces[slot] = state + kv_pieces[source_rows_s[1, sub, at]]

    def send_new(p):
        renew(p)
        new_copy(p).start()

    each_peer(send_new)
    renew(me)
    own_new_copy = fetch(part(new_pieces, me), strip(new_cache, me), 15)

    own_hit_copy.wait()
    await_all(hit_pieces, hit_recv, other_pieces)
    lane_wide = lax.broadcasted_iota(jnp.int32, (length, LANES), 1)

    def carry_in(r, sums):
        total = jnp.zeros((length, 1), F32)
        for h in range(head_count):
            cols = slice(h * size, (h + 1) * size)
            state = prefix[r, h * size : (h + 1) * size, :]
            state_high = state.astype(BF16)
            state_low = (state - state_high.astype(F32)).astype(BF16)
            q = queries[r, :, cols]
            carried = jnp.dot(q, state_high, preferred_element_type=F32)
            carried = carried + jnp.dot(q, state_low, preferred_element_type=F32)
            out = heads[r, :, cols] + carried * decay_cols[r, :, cols]
            heads[r, :, cols] = out
            total = total + jnp.sum(out * out, axis=1, keepdims=True)
        return jnp.where(lane_wide == r, total, sums)

    sums = lax.fori_loop(0, count, carry_in, jnp.zeros((length, LANES), F32))
    flat = jnp.transpose(sums)
    packed = jnp.concatenate([flat[0:8], flat[8:16]], axis=1)
    own_squares[...] = packed
    squares[z] = packed

    @pl.when(me != last)
    def _():
        pl.semaphore_wait(planes_in, 1)

    each_z(lambda p: square_copy(p).start())
    await_all(squares, square_recv, nz - 1)
    total = jnp.sum(squares[...], axis=0)
    inv = lax.rsqrt(total / (width * nz) + 1e-06)
    inv = jnp.transpose(inv)

    def norm(r, carry):
        low_half = jnp.sum(jnp.where(lane8 == r, inv[0:length], 0.0), axis=1, keepdims=True)
        high_half = jnp.sum(jnp.where(lane8 == r - 8, inv[length:], 0.0), axis=1, keepdims=True)
        scale = low_half + high_half
        attended[r] = (heads[r] * scale * gain[...]).astype(BF16)
        return carry

    lane8 = lax.broadcasted_iota(jnp.int32, (length, 8), 1)
    lax.fori_loop(0, count, norm, 0)

    own_new_copy.wait()
    await_all(new_pieces, new_recv, other_pieces)
    await_all(slots, slot_send, others)
    await_all(decays, decay_send, others)
    await_all(new_pieces, new_send, other_pieces)
    await_all(pieces, cache_send, other_pieces)
    await_all(kv_pieces, kv_send, other_pieces)
    await_all(hit_pieces, hit_send, other_pieces)
    await_all(squares, square_send, nz - 1)


def body(
    n, nz, queries, key_rows, values, log_decay, state_cache, norm_gain, entry_slot, hit_entry, write_entry
):
    count, length, width = queries.shape
    entries, head_count, size, _ = state_cache.shape
    tall = head_count * size
    rows = tall // n
    vmem, hbm = pl.BlockSpec(memory_space=pltpu.VMEM), pl.BlockSpec(memory_space=pltpu.HBM)
    sem = pltpu.SemaphoreType.DMA
    attended, new_cache = pl.pallas_call(
        functools.partial(kernel, n, nz),
        out_shape=(
            pltpu.VMEM((count, length, width), BF16),
            pltpu.VMEM((entries, tall, size), F32),
        ),
        in_specs=[hbm] * 9,
        out_specs=(vmem, vmem),
        scratch_shapes=[
            pltpu.VMEM((n * entries + 8, rows, size), F32),
            pltpu.VMEM((n * count + 8, rows, size), F32),
            pltpu.VMEM((count, tall, size), F32),
            pltpu.VMEM((n * count, rows, size), F32),
            pltpu.VMEM((n * entries, rows, size), F32),
            pltpu.VMEM((count, tall, size), F32),
            pltpu.VMEM((count, length, width), F32),
            pltpu.VMEM((count, length, width), F32),
            pltpu.VMEM((1, LANES), jnp.int32),
            pltpu.VMEM((n, 1, LANES), jnp.int32),
            pltpu.VMEM((1, LANES), F32),
            pltpu.VMEM((n, 1, LANES), F32),
            pltpu.VMEM((2, 8, LANES), jnp.int32),
            pltpu.VMEM((8, LANES), F32),
            pltpu.VMEM((8, LANES), F32),
            pltpu.VMEM((nz, 8, LANES), F32),
            pltpu.VMEM(log_decay.shape, F32),
            *[pltpu.VMEM((count, length, width), BF16)] * 3,
            pltpu.VMEM((1, width), F32),
            pltpu.SMEM((n, 1, LANES), jnp.int32),
            pltpu.SMEM((n, 1, LANES), F32),
            pltpu.SMEM((2, 8, LANES), jnp.int32),
            pltpu.SMEM((8, LANES), F32),
            pltpu.SMEM(entry_slot.shape, jnp.int32),
            pltpu.SMEM(hit_entry.shape, jnp.int32),
            pltpu.SMEM(write_entry.shape, jnp.int32),
            *[sem] * 14,
            sem((16,)),
            pltpu.SemaphoreType.REGULAR,
            pltpu.SemaphoreType.REGULAR,
        ],
        compiler_params=pltpu.CompilerParams(
            collective_id=0, has_side_effects=True, vmem_limit_bytes=32 << 20
        ),
    )(
        *(
            pltpu.with_memory_space_constraint(x, pltpu.HBM)
            for x in (
                entry_slot, hit_entry, write_entry, log_decay, queries, key_rows, values,
                norm_gain.reshape(1, width), state_cache.reshape(entries, tall, size),
            )
        )
    )
    return attended, new_cache.reshape(state_cache.shape)


def solution(mesh):
    placed = (
        P("req", None, "head"),
        P("req", None, "head"),
        P("req", None, "head"),
        P("req", "head", None),
        P("req", "head", None, None),
        P("head"),
        P(),
        P("req"),
        P("req"),
    )
    return jax.shard_map(
        functools.partial(body, mesh.shape["req"], mesh.shape["head"]),
        mesh=mesh,
        in_specs=placed,
        out_specs=(P("req", None, "head"), P("req", "head", None, None)),
        check_vma=False,
    )
```

```python
import functools

import jax
import jax.numpy as jnp
from jax import lax
from jax.experimental import pallas as pl
from jax.experimental.pallas import tpu as pltpu
from jax.sharding import PartitionSpec as P

MESH = pl.DeviceIdType.MESH
F32 = jnp.float32
BF16 = jnp.bfloat16
LANES = 128
HIT, WRITE = 0, 16
STRIDE = 5
UNROLL = 4


def nt(a, b, **kw):
    return lax.dot_general(a, b, (((1,), (1,)), ((), ())), preferred_element_type=F32, **kw)


def tn(a, b):
    return lax.dot_general(a, b, (((0,), (0,)), ((), ())), preferred_element_type=F32)


def kernel(
    n, nz, slot_hbm, hit_hbm, write_hbm, log_decay_hbm, queries_hbm, key_rows_hbm, values_hbm, gain_hbm, cache,
    attended, new_cache,
    pieces, kv_pieces, kv, hit_pieces, new_pieces, prefix, heads, decay_cols, own_slots, slots,
    own_decay, decays, source_rows, source_decay, own_squares, squares, log_decay, queries, key_rows, values, gain,
    slots_s, decays_s, source_rows_s, source_decay_s, entry_slot, hit_entry, write_entry,
    slot_send, slot_recv, decay_send, decay_recv, cache_send, cache_recv, kv_send, kv_recv,
    hit_send, hit_recv, new_send, new_recv, square_send, square_recv, local_sem, plane_in, planes_in,
):
    count, length, width = queries.shape
    head_count = log_decay.shape[1]
    size = width // head_count
    rows = cache.shape[1] // n
    me, z = lax.axis_index("req"), lax.axis_index("head")

    core = lax.rem(me, 2)
    y2 = lax.rem(me, 8) - core
    x8 = me - lax.rem(me, 8)

    def each_peer(act, low=1, high=n):
        def step(i, carry):
            d = lax.rem(i * STRIDE, n)
            within = lax.rem(d, 8)
            side = lax.rem(d, 2)
            act(lax.rem(x8 + d - within, n) + lax.rem(y2 + within - side, 8) + lax.rem(core + side, 2))
            return carry

        lax.fori_loop(low, high, step, 0)

    def each_z(act):
        def step(d, carry):
            act(lax.rem(z + d, nz))
            return carry

        lax.fori_loop(1, nz, step, 0)

    def remote(src, dst, send, recv, device):
        return pltpu.make_async_remote_copy(
            src_ref=src, dst_ref=dst, send_sem=send, recv_sem=recv, device_id=device, device_id_type=MESH
        )

    def part(ref, device):
        return ref.at[pl.ds(device * count, count)]

    def strip(ref, device):
        return ref.at[:, pl.ds(pl.multiple_of(device * rows, rows), rows), :]

    def slot_copy(peer):
        return remote(own_slots, slots.at[me], slot_send, slot_recv, (peer, z))

    def decay_copy(peer):
        return remote(own_decay, decays.at[me], decay_send, decay_recv, (peer, z))

    def cache_copy(peer):
        return remote(strip(cache, peer), part(pieces, me), cache_send, cache_recv, (peer, z))

    def kv_copy(peer):
        return remote(strip(kv, peer), part(kv_pieces, me), kv_send, kv_recv, (peer, z))

    def hit_copy(peer):
        return remote(part(hit_pieces, peer), strip(prefix, me), hit_send, hit_recv, (peer, z))

    def new_copy(peer):
        return remote(part(new_pieces, peer), strip(new_cache, me), new_send, new_recv, (peer, z))

    def square_copy(peer):
        return remote(own_squares, squares.at[z], square_send, square_recv, (me, peer))

    def await_all(ref, semaphore, amount):
        whole = ref.at[pl.ds(0, amount)]
        pltpu.make_async_copy(whole, whole, semaphore).wait()

    others, other_pieces = n - 1, (n - 1) * count

    barrier = pltpu.get_barrier_semaphore()
    last = n - 1

    def signal(semaphore, device):
        pl.semaphore_signal(semaphore, inc=1, device_id=device, device_id_type=MESH)

    def greet(p):
        @pl.when(p != last)
        def _():
            signal(barrier, (p, z))

    each_peer(greet)

    def fetch(src, dst, k):
        copy = pltpu.make_async_copy(src, dst, local_sem.at[k])
        copy.start()
        return copy

    tables_in = [
        fetch(hit_hbm, hit_entry, 0),
        fetch(write_hbm, write_entry, 1),
        fetch(slot_hbm, entry_slot, 2),
        fetch(log_decay_hbm, log_decay, 3),
    ]
    rows_in = [
        fetch(queries_hbm, queries, 4),
        fetch(key_rows_hbm, key_rows, 5),
        fetch(values_hbm, values, 6),
        fetch(gain_hbm, gain, 7),
    ]
    own_cache_copy = fetch(strip(cache, me), part(pieces, me), 8)
    none = n * count
    pieces[pl.ds(none, 8)] = jnp.zeros((8, rows, LANES), F32)
    kv_pieces[pl.ds(none, 8)] = jnp.zeros((8, rows, LANES), F32)

    @pl.when(me != last)
    def _():
        pl.semaphore_wait(barrier, n - 1)

    @pl.when(me == last - 1)
    def _():
        signal(plane_in, (last, z))

    @pl.when(me == last)
    def _():
        pl.semaphore_wait(plane_in, 1)
        each_z(lambda p: signal(barrier, (me, p)))

    each_peer(lambda p: cache_copy(p).start(), 1, n // 4)
    for copy in tables_in:
        copy.wait()
    lane = lax.broadcasted_iota(jnp.int32, (1, LANES), 1)
    table = jnp.zeros((1, LANES), jnp.int32)
    decay_row = jnp.zeros((1, LANES), F32)
    for r in range(count):
        hit, write = hit_entry[r], write_entry[r]
        hit_slot = jnp.where(hit >= 0, entry_slot[jnp.maximum(hit, 0)], none)
        write_slot = jnp.where(write >= 0, entry_slot[jnp.maximum(write, 0)], -1)
        table = jnp.where(lane == HIT + r, hit_slot, table)
        table = jnp.where(lane == WRITE + r, write_slot, table)
        whole = jnp.exp(jnp.sum(log_decay[r], axis=1, keepdims=True))
        for h in range(head_count):
            decay_row = jnp.where(lane == r * head_count + h, whole[h : h + 1], decay_row)
    own_slots[...] = table
    slots[me] = table
    own_decay[...] = decay_row
    decays[me] = decay_row
    each_peer(lambda p: slot_copy(p).start())
    each_peer(lambda p: decay_copy(p).start())
    each_peer(lambda p: cache_copy(p).start(), n // 4, n)
    for copy in rows_in:
        copy.wait()

    low = lax.broadcasted_iota(jnp.int32, (length, length), 0)
    col = lax.broadcasted_iota(jnp.int32, (length, length), 1)
    causal = low >= col
    lower, upper = jnp.where(causal, 1.0, 0.0), jnp.where(low <= col, 1.0, 0.0)

    def block(r, carry):
        steps = log_decay[r]
        high = dict(precision=lax.Precision.HIGHEST)
        gsum_rows = jnp.dot(steps, upper, preferred_element_type=F32, **high)
        gsum_cols = nt(lower, steps, **high)
        last = gsum_rows[:, length - 1 : length]
        grown = jnp.exp(gsum_cols)
        for h in range(head_count):
            cols = slice(h * size, (h + 1) * size)
            q, k, v = queries[r, :, cols], key_rows[r, :, cols], values[r, :, cols]
            gcol, grow, glast = gsum_cols[:, h : h + 1], gsum_rows[h : h + 1], last[h : h + 1]
            gap = jnp.where(causal, jnp.exp(jnp.minimum(gcol - grow, 0.0)), 0.0)
            weights = (nt(q, k) * gap).astype(BF16)
            heads[r, :, cols] = jnp.dot(weights, v, preferred_element_type=F32)
            weighted = (k.astype(F32) * jnp.exp(glast - gcol)).astype(BF16)
            kv[r, h * size : (h + 1) * size, :] = tn(weighted, v)
            decay_cols[r, :, cols] = jnp.broadcast_to(grown[:, h : h + 1], (length, size))
        return carry

    lax.fori_loop(0, count, block, 0)
    own_kv_copy = fetch(strip(kv, me), part(kv_pieces, me), 13)

    each_peer(lambda p: kv_copy(p).start())

    await_all(slots, slot_recv, others)
    await_all(decays, decay_recv, others)
    for copy in [fetch(slots, slots_s, 9), fetch(decays, decays_s, 10)]:
        copy.wait()
    place = (
        lax.broadcasted_iota(jnp.int32, (8, LANES), 0) * LANES
        + lax.broadcasted_iota(jnp.int32, (8, LANES), 1)
    )
    my_head = (me * rows) // size

    def invert(device, found):
        hit_row, kv_row, decay = found
        for r in range(count):
            here = place == slots_s[device, 0, WRITE + r]
            hit_row = jnp.where(here, slots_s[device, 0, HIT + r], hit_row)
            kv_row = jnp.where(here, device * count + r, kv_row)
            decay = jnp.where(here, decays_s[device, 0, r * head_count + my_head], decay)
        return hit_row, kv_row, decay

    hit_row, kv_row, decay = lax.fori_loop(
        0, n, invert, (place, jnp.full((8, LANES), none, jnp.int32), jnp.ones((8, LANES), F32))
    )
    source_rows[0] = hit_row
    source_rows[1] = kv_row
    source_decay[...] = decay
    sources_in = [fetch(source_rows, source_rows_s, 11), fetch(source_decay, source_decay_s, 12)]


    own_cache_copy.wait()
    await_all(pieces, cache_recv, other_pieces)

    def pick(device):
        for r in range(count):
            hit_pieces[device * count + r] = pieces[slots_s[device, 0, HIT + r]]

    def send_hits(p):
        pick(p)
        hit_copy(p).start()

    each_peer(send_hits)
    pick(me)
    own_hit_copy = fetch(part(hit_pieces, me), strip(prefix, me), 14)

    @pl.when(me == last)
    def _():
        pl.semaphore_wait(barrier, nz - 1)
        each_peer(lambda p: signal(planes_in, (p, z)))

    own_kv_copy.wait()
    await_all(kv_pieces, kv_recv, other_pieces)
    for copy in sources_in:
        copy.wait()

    def renew(device):
        for e in range(count):
            slot = device * count + e
            sub, at = lax.div(slot, LANES), lax.rem(slot, LANES)
            state = source_decay_s[sub, at] * pieces[source_rows_s[0, sub, at]]
            new_pieces[slot] = state + kv_pieces[source_rows_s[1, sub, at]]

    def send_new(p):
        renew(p)
        new_copy(p).start()

    each_peer(send_new)
    renew(me)
    own_new_copy = fetch(part(new_pieces, me), strip(new_cache, me), 15)

    own_hit_copy.wait()
    await_all(hit_pieces, hit_recv, other_pieces)
    lane_wide = lax.broadcasted_iota(jnp.int32, (length, LANES), 1)

    def carry_in(r, sums):
        total = jnp.zeros((length, 1), F32)
        for h in range(head_count):
            cols = slice(h * size, (h + 1) * size)
            state = prefix[r, h * size : (h + 1) * size, :]
            state_high = state.astype(BF16)
            state_low = (state - state_high.astype(F32)).astype(BF16)
            q = queries[r, :, cols]
            carried = jnp.dot(q, state_high, preferred_element_type=F32)
            carried = carried + jnp.dot(q, state_low, preferred_element_type=F32)
            out = heads[r, :, cols] + carried * decay_cols[r, :, cols]
            heads[r, :, cols] = out
            total = total + jnp.sum(out * out, axis=1, keepdims=True)
        return jnp.where(lane_wide == r, total, sums)

    sums = lax.fori_loop(0, count, carry_in, jnp.zeros((length, LANES), F32), unroll=UNROLL)
    flat = jnp.transpose(sums)
    packed = jnp.concatenate([flat[0:8], flat[8:16]], axis=1)
    own_squares[...] = packed
    squares[z] = packed

    @pl.when(me != last)
    def _():
        pl.semaphore_wait(planes_in, 1)

    each_z(lambda p: square_copy(p).start())
    await_all(squares, square_recv, nz - 1)
    total = jnp.sum(squares[...], axis=0)
    inv = lax.rsqrt(total / (width * nz) + 1e-06)
    inv = jnp.transpose(inv)

    wide_gain = jnp.broadcast_to(gain[...], (length, width))
    for r in range(count):
        down, at = (r // 8) * length, r % 8
        scale = jnp.broadcast_to(inv[down : down + length, at : at + 1], (length, width))
        attended[r] = (heads[r] * scale * wide_gain).astype(BF16)

    own_new_copy.wait()
    await_all(new_pieces, new_recv, other_pieces)
    await_all(slots, slot_send, others)
    await_all(decays, decay_send, others)
    await_all(new_pieces, new_send, other_pieces)
    await_all(pieces, cache_send, other_pieces)
    await_all(kv_pieces, kv_send, other_pieces)
    await_all(hit_pieces, hit_send, other_pieces)
    await_all(squares, square_send, nz - 1)


def write_out(attended, new_cache, attended_out, new_cache_out, done):
    quarter = new_cache.shape[0] // 4
    copies = [pltpu.make_async_copy(attended, attended_out, done.at[4])]
    for k in range(4):
        part = pl.ds(k * quarter, quarter)
        copies.append(pltpu.make_async_copy(new_cache.at[part], new_cache_out.at[part], done.at[k]))
    for copy in copies:
        copy.start()
    for copy in copies:
        copy.wait()


def body(
    n, nz, queries, key_rows, values, log_decay, state_cache, norm_gain, entry_slot, hit_entry, write_entry
):
    count, length, width = queries.shape
    entries, head_count, size, _ = state_cache.shape
    tall = head_count * size
    rows = tall // n
    vmem, hbm = pl.BlockSpec(memory_space=pltpu.VMEM), pl.BlockSpec(memory_space=pltpu.HBM)
    sem = pltpu.SemaphoreType.DMA
    attended, new_cache = pl.pallas_call(
        functools.partial(kernel, n, nz),
        out_shape=(
            pltpu.VMEM((count, length, width), BF16),
            pltpu.VMEM((entries, tall, size), F32),
        ),
        in_specs=[hbm] * 9,
        out_specs=(vmem, vmem),
        scratch_shapes=[
            pltpu.VMEM((n * entries + 8, rows, size), F32),
            pltpu.VMEM((n * count + 8, rows, size), F32),
            pltpu.VMEM((count, tall, size), F32),
            pltpu.VMEM((n * count, rows, size), F32),
            pltpu.VMEM((n * entries, rows, size), F32),
            pltpu.VMEM((count, tall, size), F32),
            pltpu.VMEM((count, length, width), F32),
            pltpu.VMEM((count, length, width), F32),
            pltpu.VMEM((1, LANES), jnp.int32),
            pltpu.VMEM((n, 1, LANES), jnp.int32),
            pltpu.VMEM((1, LANES), F32),
            pltpu.VMEM((n, 1, LANES), F32),
            pltpu.VMEM((2, 8, LANES), jnp.int32),
            pltpu.VMEM((8, LANES), F32),
            pltpu.VMEM((8, LANES), F32),
            pltpu.VMEM((nz, 8, LANES), F32),
            pltpu.VMEM(log_decay.shape, F32),
            *[pltpu.VMEM((count, length, width), BF16)] * 3,
            pltpu.VMEM((1, width), F32),
            pltpu.SMEM((n, 1, LANES), jnp.int32),
            pltpu.SMEM((n, 1, LANES), F32),
            pltpu.SMEM((2, 8, LANES), jnp.int32),
            pltpu.SMEM((8, LANES), F32),
            pltpu.SMEM(entry_slot.shape, jnp.int32),
            pltpu.SMEM(hit_entry.shape, jnp.int32),
            pltpu.SMEM(write_entry.shape, jnp.int32),
            *[sem] * 14,
            sem((16,)),
            pltpu.SemaphoreType.REGULAR,
            pltpu.SemaphoreType.REGULAR,
        ],
        compiler_params=pltpu.CompilerParams(
            collective_id=0, has_side_effects=True, vmem_limit_bytes=32 << 20
        ),
    )(
        *(
            pltpu.with_memory_space_constraint(x, pltpu.HBM)
            for x in (
                entry_slot, hit_entry, write_entry, log_decay, queries, key_rows, values,
                norm_gain.reshape(1, width), state_cache.reshape(entries, tall, size),
            )
        )
    )
    attended, new_cache = pl.pallas_call(
        write_out,
        out_shape=(
            jax.ShapeDtypeStruct((count, length, width), BF16),
            jax.ShapeDtypeStruct((entries, tall, size), F32),
        ),
        in_specs=[vmem, vmem],
        out_specs=(pl.BlockSpec(memory_space=pl.ANY),) * 2,
        scratch_shapes=[sem((5,))],
    )(*(pltpu.with_memory_space_constraint(a, pltpu.VMEM) for a in (attended, new_cache)))
    return attended, new_cache.reshape(state_cache.shape)


def solution(mesh):
    placed = (
        P("req", None, "head"),
        P("req", None, "head"),
        P("req", None, "head"),
        P("req", "head", None),
        P("req", "head", None, None),
        P("head"),
        P(),
        P("req"),
        P("req"),
    )
    return jax.shard_map(
        functools.partial(body, mesh.shape["req"], mesh.shape["head"]),
        mesh=mesh,
        in_specs=placed,
        out_specs=(P("req", None, "head"), P("req", "head", None, None)),
        check_vma=False,
    )
```

```python
import functools

import jax
import jax.numpy as jnp
from jax import lax
from jax.experimental import pallas as pl
from jax.experimental.pallas import tpu as pltpu
from jax.sharding import PartitionSpec as P

MESH = pl.DeviceIdType.MESH
F32 = jnp.float32
BF16 = jnp.bfloat16
LANES = 128
HIT, WRITE = 0, 16
STRIDE = 5
LATE = 6
UNROLL = 4


def nt(a, b, **kw):
    return lax.dot_general(a, b, (((1,), (1,)), ((), ())), preferred_element_type=F32, **kw)


def tn(a, b):
    return lax.dot_general(a, b, (((0,), (0,)), ((), ())), preferred_element_type=F32)


def kernel(
    n, nz, slot_hbm, hit_hbm, write_hbm, log_decay_hbm, queries_hbm, key_rows_hbm, values_hbm, gain_hbm, cache,
    attended, new_cache,
    pieces, kv_pieces, kv, hit_pieces, new_pieces, prefix, heads, decay_cols, own_slots, slots,
    own_decay, decays, source_rows, source_decay, own_squares, squares, log_decay, queries, key_rows, values, gain,
    slots_s, decays_s, source_rows_s, source_decay_s, entry_slot, hit_entry, write_entry,
    slot_send, slot_recv, decay_send, decay_recv, cache_send, cache_recv, kv_send, kv_recv,
    hit_send, hit_recv, new_send, new_recv, square_send, square_recv, local_sem, plane_in, planes_in, first_in,
):
    count, length, width = queries.shape
    head_count = log_decay.shape[1]
    size = width // head_count
    rows = cache.shape[1] // n
    me, z = lax.axis_index("req"), lax.axis_index("head")

    core = lax.rem(me, 2)
    y2 = lax.rem(me, 8) - core
    x8 = me - lax.rem(me, 8)

    def each_peer(act, low=1, high=n):
        def step(i, carry):
            d = lax.rem(i * STRIDE, n)
            within = lax.rem(d, 8)
            side = lax.rem(d, 2)
            act(lax.rem(x8 + d - within, n) + lax.rem(y2 + within - side, 8) + lax.rem(core + side, 2))
            return carry

        lax.fori_loop(low, high, step, 0)

    def each_z(act):
        def step(d, carry):
            act(lax.rem(z + d, nz))
            return carry

        lax.fori_loop(1, nz, step, 0)

    def remote(src, dst, send, recv, device):
        return pltpu.make_async_remote_copy(
            src_ref=src, dst_ref=dst, send_sem=send, recv_sem=recv, device_id=device, device_id_type=MESH
        )

    def part(ref, device):
        return ref.at[pl.ds(device * count, count)]

    def strip(ref, device):
        return ref.at[:, pl.ds(pl.multiple_of(device * rows, rows), rows), :]

    def slot_copy(peer):
        return remote(own_slots, slots.at[me], slot_send, slot_recv, (peer, z))

    def decay_copy(peer):
        return remote(own_decay, decays.at[me], decay_send, decay_recv, (peer, z))

    def cache_copy(peer):
        return remote(strip(cache, peer), part(pieces, me), cache_send, cache_recv, (peer, z))

    def kv_copy(peer):
        return remote(strip(kv, peer), part(kv_pieces, me), kv_send, kv_recv, (peer, z))

    def hit_copy(peer):
        return remote(part(hit_pieces, peer), strip(prefix, me), hit_send, hit_recv, (peer, z))

    def new_copy(peer):
        return remote(part(new_pieces, peer), strip(new_cache, me), new_send, new_recv, (peer, z))

    def square_copy(peer):
        return remote(own_squares, squares.at[z], square_send, square_recv, (me, peer))

    def await_all(ref, semaphore, amount):
        whole = ref.at[pl.ds(0, amount)]
        pltpu.make_async_copy(whole, whole, semaphore).wait()

    others, other_pieces = n - 1, (n - 1) * count

    barrier = pltpu.get_barrier_semaphore()
    first, last = 0, n - 1
    waits_late = z == 0

    def each_in_time(act, low=1, high=n):
        def step(p):
            @pl.when((p != first) | jnp.logical_not(waits_late))
            def _():
                act(p)

        each_peer(step, low, high)

    def signal(semaphore, device):
        pl.semaphore_signal(semaphore, inc=1, device_id=device, device_id_type=MESH)

    def greet(p):
        @pl.when(p != last)
        def _():
            signal(barrier, (p, z))

    @pl.when((me != first) | jnp.logical_not(waits_late))
    def _():
        for i in range(1, n):
            d = i * STRIDE % n
            greet(lax.rem(x8 + d // 8 * 8, n) + lax.rem(y2 + d // 2 % 4 * 2, 8) + lax.rem(core + d % 2, 2))

    def fetch(src, dst, k):
        copy = pltpu.make_async_copy(src, dst, local_sem.at[k])
        copy.start()
        return copy

    tables_in = [
        fetch(hit_hbm, hit_entry, 0),
        fetch(write_hbm, write_entry, 1),
        fetch(slot_hbm, entry_slot, 2),
        fetch(log_decay_hbm, log_decay, 3),
    ]
    rows_in = [
        fetch(queries_hbm, queries, 4),
        fetch(key_rows_hbm, key_rows, 5),
        fetch(values_hbm, values, 6),
        fetch(gain_hbm, gain, 7),
    ]
    own_cache_copy = fetch(strip(cache, me), part(pieces, me), 8)
    none = n * count

    @pl.when(me == first)
    def _():
        pl.semaphore_wait(barrier, n - 1)

        @pl.when(waits_late)
        def _():
            each_peer(lambda p: signal(first_in, (p, z)))

    @pl.when((me != first) & (me != last))
    def _():
        pl.semaphore_wait(barrier, n - 1 - jnp.where(waits_late, 1, 0))

    @pl.when(me == last - 1)
    def _():
        signal(plane_in, (last, z))

    @pl.when(me == last)
    def _():
        pl.semaphore_wait(plane_in, 1)

    each_in_time(lambda p: cache_copy(p).start(), 1, n // 4)
    pieces[pl.ds(none, 8)] = jnp.zeros((8, rows, LANES), F32)
    kv_pieces[pl.ds(none, 8)] = jnp.zeros((8, rows, LANES), F32)
    for copy in tables_in:
        copy.wait()
    lane = lax.broadcasted_iota(jnp.int32, (1, LANES), 1)
    table = jnp.zeros((1, LANES), jnp.int32)
    decay_row = jnp.zeros((1, LANES), F32)
    for r in range(count):
        hit, write = hit_entry[r], write_entry[r]
        hit_slot = jnp.where(hit >= 0, entry_slot[jnp.maximum(hit, 0)], none)
        write_slot = jnp.where(write >= 0, entry_slot[jnp.maximum(write, 0)], -1)
        table = jnp.where(lane == HIT + r, hit_slot, table)
        table = jnp.where(lane == WRITE + r, write_slot, table)
        whole = jnp.exp(jnp.sum(log_decay[r], axis=1, keepdims=True))
        for h in range(head_count):
            decay_row = jnp.where(lane == r * head_count + h, whole[h : h + 1], decay_row)
    own_slots[...] = table
    slots[me] = table
    own_decay[...] = decay_row
    decays[me] = decay_row
    each_in_time(lambda p: slot_copy(p).start())
    each_in_time(lambda p: decay_copy(p).start())
    each_in_time(lambda p: cache_copy(p).start(), n // 4, n)
    for copy in rows_in:
        copy.wait()

    low = lax.broadcasted_iota(jnp.int32, (length, length), 0)
    col = lax.broadcasted_iota(jnp.int32, (length, length), 1)
    causal = low >= col
    lower, upper = jnp.where(causal, 1.0, 0.0), jnp.where(low <= col, 1.0, 0.0)

    def block(r, carry):
        @pl.when(waits_late & (me != first) & (r == LATE + lax.rem(me, count - LATE)))
        def _():
            pl.semaphore_wait(first_in, 1)
            slot_copy(first).start()
            decay_copy(first).start()
            cache_copy(first).start()

        steps = log_decay[r]
        high = dict(precision=lax.Precision.HIGHEST)
        gsum_rows = jnp.dot(steps, upper, preferred_element_type=F32, **high)
        gsum_cols = nt(lower, steps, **high)
        last = gsum_rows[:, length - 1 : length]
        grown = jnp.exp(gsum_cols)
        for h in range(head_count):
            cols = slice(h * size, (h + 1) * size)
            q, k, v = queries[r, :, cols], key_rows[r, :, cols], values[r, :, cols]
            gcol, grow, glast = gsum_cols[:, h : h + 1], gsum_rows[h : h + 1], last[h : h + 1]
            gap = jnp.where(causal, jnp.exp(jnp.minimum(gcol - grow, 0.0)), 0.0)
            weights = (nt(q, k) * gap).astype(BF16)
            heads[r, :, cols] = jnp.dot(weights, v, preferred_element_type=F32)
            weighted = (k.astype(F32) * jnp.exp(glast - gcol)).astype(BF16)
            kv[r, h * size : (h + 1) * size, :] = tn(weighted, v)
            decay_cols[r, :, cols] = jnp.broadcast_to(grown[:, h : h + 1], (length, size))
        return carry

    lax.fori_loop(0, count, block, 0)

    @pl.when(me == last)
    def _():
        each_z(lambda p: signal(barrier, (me, p)))

    own_kv_copy = fetch(strip(kv, me), part(kv_pieces, me), 13)

    each_peer(lambda p: kv_copy(p).start())

    await_all(slots, slot_recv, others)
    await_all(decays, decay_recv, others)
    for copy in [fetch(slots, slots_s, 9), fetch(decays, decays_s, 10)]:
        copy.wait()
    place = (
        lax.broadcasted_iota(jnp.int32, (8, LANES), 0) * LANES
        + lax.broadcasted_iota(jnp.int32, (8, LANES), 1)
    )
    my_head = (me * rows) // size

    def invert(device, found):
        hit_row, kv_row, decay = found
        for r in range(count):
            here = place == slots_s[device, 0, WRITE + r]
            hit_row = jnp.where(here, slots_s[device, 0, HIT + r], hit_row)
            kv_row = jnp.where(here, device * count + r, kv_row)
            decay = jnp.where(here, decays_s[device, 0, r * head_count + my_head], decay)
        return hit_row, kv_row, decay

    hit_row, kv_row, decay = lax.fori_loop(
        0, n, invert, (place, jnp.full((8, LANES), none, jnp.int32), jnp.ones((8, LANES), F32))
    )
    source_rows[0] = hit_row
    source_rows[1] = kv_row
    source_decay[...] = decay
    sources_in = [fetch(source_rows, source_rows_s, 11), fetch(source_decay, source_decay_s, 12)]


    own_cache_copy.wait()
    await_all(pieces, cache_recv, other_pieces)

    def pick(device):
        for r in range(count):
            hit_pieces[device * count + r] = pieces[slots_s[device, 0, HIT + r]]

    def send_hits(p):
        pick(p)
        hit_copy(p).start()

    each_peer(send_hits)
    pick(me)
    own_hit_copy = fetch(part(hit_pieces, me), strip(prefix, me), 14)

    @pl.when(me == last)
    def _():
        pl.semaphore_wait(barrier, nz - 1)
        each_peer(lambda p: signal(planes_in, (p, z)))

    own_kv_copy.wait()
    await_all(kv_pieces, kv_recv, other_pieces)
    for copy in sources_in:
        copy.wait()

    def renew(device):
        for e in range(count):
            slot = device * count + e
            sub, at = lax.div(slot, LANES), lax.rem(slot, LANES)
            state = source_decay_s[sub, at] * pieces[source_rows_s[0, sub, at]]
            new_pieces[slot] = state + kv_pieces[source_rows_s[1, sub, at]]

    def send_new(p):
        renew(p)
        new_copy(p).start()

    each_peer(send_new)
    renew(me)
    own_new_copy = fetch(part(new_pieces, me), strip(new_cache, me), 15)

    own_hit_copy.wait()
    await_all(hit_pieces, hit_recv, other_pieces)
    lane_wide = lax.broadcasted_iota(jnp.int32, (length, LANES), 1)

    def carry_in(r, sums):
        total = jnp.zeros((length, 1), F32)
        for h in range(head_count):
            cols = slice(h * size, (h + 1) * size)
            state = prefix[r, h * size : (h + 1) * size, :]
            state_high = state.astype(BF16)
            state_low = (state - state_high.astype(F32)).astype(BF16)
            q = queries[r, :, cols]
            carried = jnp.dot(q, state_high, preferred_element_type=F32)
            carried = carried + jnp.dot(q, state_low, preferred_element_type=F32)
            out = heads[r, :, cols] + carried * decay_cols[r, :, cols]
            heads[r, :, cols] = out
            total = total + jnp.sum(out * out, axis=1, keepdims=True)
        return jnp.where(lane_wide == r, total, sums)

    sums = lax.fori_loop(0, count, carry_in, jnp.zeros((length, LANES), F32), unroll=UNROLL)
    flat = jnp.transpose(sums)
    packed = jnp.concatenate([flat[0:8], flat[8:16]], axis=1)
    own_squares[...] = packed
    squares[z] = packed

    @pl.when(me != last)
    def _():
        pl.semaphore_wait(planes_in, 1)

    each_z(lambda p: square_copy(p).start())
    await_all(squares, square_recv, nz - 1)
    total = jnp.sum(squares[...], axis=0)
    inv = lax.rsqrt(total / (width * nz) + 1e-06)
    inv = jnp.transpose(inv)

    wide_gain = jnp.broadcast_to(gain[...], (length, width))
    for r in range(count):
        down, at = (r // 8) * length, r % 8
        scale = jnp.broadcast_to(inv[down : down + length, at : at + 1], (length, width))
        attended[r] = (heads[r] * scale * wide_gain).astype(BF16)

    own_new_copy.wait()
    await_all(new_pieces, new_recv, other_pieces)
    await_all(slots, slot_send, others)
    await_all(decays, decay_send, others)
    await_all(new_pieces, new_send, other_pieces)
    await_all(pieces, cache_send, other_pieces)
    await_all(kv_pieces, kv_send, other_pieces)
    await_all(hit_pieces, hit_send, other_pieces)
    await_all(squares, square_send, nz - 1)


def write_out(attended, new_cache, attended_out, new_cache_out, done):
    quarter = new_cache.shape[0] // 4
    copies = [pltpu.make_async_copy(attended, attended_out, done.at[4])]
    for k in range(4):
        part = pl.ds(k * quarter, quarter)
        copies.append(pltpu.make_async_copy(new_cache.at[part], new_cache_out.at[part], done.at[k]))
    for copy in copies:
        copy.start()
    for copy in copies:
        copy.wait()


def body(
    n, nz, queries, key_rows, values, log_decay, state_cache, norm_gain, entry_slot, hit_entry, write_entry
):
    count, length, width = queries.shape
    entries, head_count, size, _ = state_cache.shape
    tall = head_count * size
    rows = tall // n
    vmem, hbm = pl.BlockSpec(memory_space=pltpu.VMEM), pl.BlockSpec(memory_space=pltpu.HBM)
    sem = pltpu.SemaphoreType.DMA
    attended, new_cache = pl.pallas_call(
        functools.partial(kernel, n, nz),
        out_shape=(
            pltpu.VMEM((count, length, width), BF16),
            pltpu.VMEM((entries, tall, size), F32),
        ),
        in_specs=[hbm] * 9,
        out_specs=(vmem, vmem),
        scratch_shapes=[
            pltpu.VMEM((n * entries + 8, rows, size), F32),
            pltpu.VMEM((n * count + 8, rows, size), F32),
            pltpu.VMEM((count, tall, size), F32),
            pltpu.VMEM((n * count, rows, size), F32),
            pltpu.VMEM((n * entries, rows, size), F32),
            pltpu.VMEM((count, tall, size), F32),
            pltpu.VMEM((count, length, width), F32),
            pltpu.VMEM((count, length, width), F32),
            pltpu.VMEM((1, LANES), jnp.int32),
            pltpu.VMEM((n, 1, LANES), jnp.int32),
            pltpu.VMEM((1, LANES), F32),
            pltpu.VMEM((n, 1, LANES), F32),
            pltpu.VMEM((2, 8, LANES), jnp.int32),
            pltpu.VMEM((8, LANES), F32),
            pltpu.VMEM((8, LANES), F32),
            pltpu.VMEM((nz, 8, LANES), F32),
            pltpu.VMEM(log_decay.shape, F32),
            *[pltpu.VMEM((count, length, width), BF16)] * 3,
            pltpu.VMEM((1, width), F32),
            pltpu.SMEM((n, 1, LANES), jnp.int32),
            pltpu.SMEM((n, 1, LANES), F32),
            pltpu.SMEM((2, 8, LANES), jnp.int32),
            pltpu.SMEM((8, LANES), F32),
            pltpu.SMEM(entry_slot.shape, jnp.int32),
            pltpu.SMEM(hit_entry.shape, jnp.int32),
            pltpu.SMEM(write_entry.shape, jnp.int32),
            *[sem] * 14,
            sem((16,)),
            *[pltpu.SemaphoreType.REGULAR] * 3,
        ],
        compiler_params=pltpu.CompilerParams(
            collective_id=0, has_side_effects=True, vmem_limit_bytes=32 << 20
        ),
    )(
        *(
            pltpu.with_memory_space_constraint(x, pltpu.HBM)
            for x in (
                entry_slot, hit_entry, write_entry, log_decay, queries, key_rows, values,
                norm_gain.reshape(1, width), state_cache.reshape(entries, tall, size),
            )
        )
    )
    attended, new_cache = pl.pallas_call(
        write_out,
        out_shape=(
            jax.ShapeDtypeStruct((count, length, width), BF16),
            jax.ShapeDtypeStruct((entries, tall, size), F32),
        ),
        in_specs=[vmem, vmem],
        out_specs=(pl.BlockSpec(memory_space=pl.ANY),) * 2,
        scratch_shapes=[sem((5,))],
    )(*(pltpu.with_memory_space_constraint(a, pltpu.VMEM) for a in (attended, new_cache)))
    return attended, new_cache.reshape(state_cache.shape)


def solution(mesh):
    placed = (
        P("req", None, "head"),
        P("req", None, "head"),
        P("req", None, "head"),
        P("req", "head", None),
        P("req", "head", None, None),
        P("head"),
        P(),
        P("req"),
        P("req"),
    )
    return jax.shard_map(
        functools.partial(body, mesh.shape["req"], mesh.shape["head"]),
        mesh=mesh,
        in_specs=placed,
        out_specs=(P("req", None, "head"), P("req", "head", None, None)),
        check_vma=False,
    )
```

```python
import functools

import jax
import jax.numpy as jnp
from jax import lax
from jax.experimental import pallas as pl
from jax.experimental.pallas import tpu as pltpu
from jax.sharding import PartitionSpec as P

MESH = pl.DeviceIdType.MESH
F32 = jnp.float32
BF16 = jnp.bfloat16
LANES = 128
HIT, WRITE = 0, 16
STRIDE = 5
LATE = 6
UNROLL = 4


def nt(a, b, **kw):
    return lax.dot_general(a, b, (((1,), (1,)), ((), ())), preferred_element_type=F32, **kw)


def tn(a, b):
    return lax.dot_general(a, b, (((0,), (0,)), ((), ())), preferred_element_type=F32)


def kernel(
    n, nz, slot_hbm, hit_hbm, write_hbm, log_decay_hbm, queries_hbm, key_rows_hbm, values_hbm, gain_hbm, cache,
    attended, new_cache,
    pieces, kv_pieces, kv, hit_pieces, new_pieces, prefix, heads, decay_cols, own_slots, slots,
    own_decay, decays, source_rows, source_decay, own_squares, squares, log_decay, queries, key_rows, values, gain,
    slots_s, decays_s, source_rows_s, source_decay_s, entry_slot, hit_entry, write_entry,
    slot_send, slot_recv, decay_send, decay_recv, cache_send, cache_recv, kv_send, kv_recv,
    hit_send, hit_recv, new_send, new_recv, square_send, square_recv, local_sem, plane_in, planes_in, first_in,
):
    count, length, width = queries.shape
    head_count = log_decay.shape[1]
    size = width // head_count
    rows = cache.shape[1] // n
    me, z = lax.axis_index("req"), lax.axis_index("head")

    core = lax.rem(me, 2)
    y2 = lax.rem(me, 8) - core
    x8 = me - lax.rem(me, 8)

    def each_peer(act, low=1, high=n):
        def step(i, carry):
            d = lax.rem(i * STRIDE, n)
            within = lax.rem(d, 8)
            side = lax.rem(d, 2)
            act(lax.rem(x8 + d - within, n) + lax.rem(y2 + within - side, 8) + lax.rem(core + side, 2))
            return carry

        lax.fori_loop(low, high, step, 0)

    def each_z(act):
        def step(d, carry):
            act(lax.rem(z + d, nz))
            return carry

        lax.fori_loop(1, nz, step, 0)

    def remote(src, dst, send, recv, device):
        return pltpu.make_async_remote_copy(
            src_ref=src, dst_ref=dst, send_sem=send, recv_sem=recv, device_id=device, device_id_type=MESH
        )

    def part(ref, device):
        return ref.at[pl.ds(device * count, count)]

    def strip(ref, device):
        return ref.at[:, pl.ds(pl.multiple_of(device * rows, rows), rows), :]

    def slot_copy(peer):
        return remote(own_slots, slots.at[me], slot_send, slot_recv, (peer, z))

    def decay_copy(peer):
        return remote(own_decay, decays.at[me], decay_send, decay_recv, (peer, z))

    def cache_copy(peer):
        return remote(strip(cache, peer), part(pieces, me), cache_send, cache_recv, (peer, z))

    def kv_copy(peer):
        return remote(strip(kv, peer), part(kv_pieces, me), kv_send, kv_recv, (peer, z))

    def hit_copy(peer):
        return remote(part(hit_pieces, peer), strip(prefix, me), hit_send, hit_recv, (peer, z))

    def new_copy(peer):
        return remote(part(new_pieces, peer), strip(new_cache, me), new_send, new_recv, (peer, z))

    def square_copy(peer):
        return remote(own_squares, squares.at[z], square_send, square_recv, (me, peer))

    def await_all(ref, semaphore, amount):
        whole = ref.at[pl.ds(0, amount)]
        pltpu.make_async_copy(whole, whole, semaphore).wait()

    others, other_pieces = n - 1, (n - 1) * count

    barrier = pltpu.get_barrier_semaphore()
    first, last = 0, n - 1
    waits_late = z == 0

    def each_in_time(act, low=1, high=n):
        def step(p):
            @pl.when((p != first) | jnp.logical_not(waits_late))
            def _():
                act(p)

        each_peer(step, low, high)

    def signal(semaphore, device):
        pl.semaphore_signal(semaphore, inc=1, device_id=device, device_id_type=MESH)

    def each_static(act):
        for i in range(1, n):
            d = i * STRIDE % n
            act(lax.rem(x8 + d // 8 * 8, n) + lax.rem(y2 + d // 2 % 4 * 2, 8) + lax.rem(core + d % 2, 2))

    def greet(p):
        @pl.when(p != last)
        def _():
            signal(barrier, (p, z))

    @pl.when((me != first) | jnp.logical_not(waits_late))
    def _():
        each_static(greet)

    def fetch(src, dst, k):
        copy = pltpu.make_async_copy(src, dst, local_sem.at[k])
        copy.start()
        return copy

    tables_in = [
        fetch(hit_hbm, hit_entry, 0),
        fetch(write_hbm, write_entry, 1),
        fetch(slot_hbm, entry_slot, 2),
        fetch(log_decay_hbm, log_decay, 3),
    ]
    none = n * count

    @pl.when(me == first)
    def _():
        pl.semaphore_wait(barrier, n - 1)

    @pl.when((me != first) & (me != last))
    def _():
        pl.semaphore_wait(barrier, n - 1 - jnp.where(waits_late, 1, 0))

    @pl.when(me == last - 1)
    def _():
        signal(plane_in, (last, z))

    @pl.when(me == last)
    def _():
        pl.semaphore_wait(plane_in, 1)

    each_in_time(lambda p: cache_copy(p).start(), 1, n // 4)

    @pl.when((me == first) & waits_late)
    def _():
        each_static(lambda p: signal(first_in, (p, z)))

    rows_in = [
        fetch(queries_hbm, queries, 4),
        fetch(key_rows_hbm, key_rows, 5),
        fetch(values_hbm, values, 6),
        fetch(gain_hbm, gain, 7),
    ]
    own_cache_copy = fetch(strip(cache, me), part(pieces, me), 8)
    pieces[pl.ds(none, 8)] = jnp.zeros((8, rows, LANES), F32)
    kv_pieces[pl.ds(none, 8)] = jnp.zeros((8, rows, LANES), F32)
    for copy in tables_in:
        copy.wait()
    lane = lax.broadcasted_iota(jnp.int32, (1, LANES), 1)
    table = jnp.zeros((1, LANES), jnp.int32)
    decay_row = jnp.zeros((1, LANES), F32)
    for r in range(count):
        hit, write = hit_entry[r], write_entry[r]
        hit_slot = jnp.where(hit >= 0, entry_slot[jnp.maximum(hit, 0)], none)
        write_slot = jnp.where(write >= 0, entry_slot[jnp.maximum(write, 0)], -1)
        table = jnp.where(lane == HIT + r, hit_slot, table)
        table = jnp.where(lane == WRITE + r, write_slot, table)
        whole = jnp.exp(jnp.sum(log_decay[r], axis=1, keepdims=True))
        for h in range(head_count):
            decay_row = jnp.where(lane == r * head_count + h, whole[h : h + 1], decay_row)
    own_slots[...] = table
    slots[me] = table
    own_decay[...] = decay_row
    decays[me] = decay_row
    each_in_time(lambda p: slot_copy(p).start())
    each_in_time(lambda p: decay_copy(p).start())
    each_in_time(lambda p: cache_copy(p).start(), n // 4, n)
    for copy in rows_in:
        copy.wait()

    low = lax.broadcasted_iota(jnp.int32, (length, length), 0)
    col = lax.broadcasted_iota(jnp.int32, (length, length), 1)
    causal = low >= col
    lower, upper = jnp.where(causal, 1.0, 0.0), jnp.where(low <= col, 1.0, 0.0)

    def block(r, carry):
        @pl.when(waits_late & (me != first) & (r == LATE + lax.rem(me, count - LATE)))
        def _():
            pl.semaphore_wait(first_in, 1)
            slot_copy(first).start()
            decay_copy(first).start()
            cache_copy(first).start()

        steps = log_decay[r]
        high = dict(precision=lax.Precision.HIGHEST)
        gsum_rows = jnp.dot(steps, upper, preferred_element_type=F32, **high)
        gsum_cols = nt(lower, steps, **high)
        last = gsum_rows[:, length - 1 : length]
        grown = jnp.exp(gsum_cols)
        for h in range(head_count):
            cols = slice(h * size, (h + 1) * size)
            q, k, v = queries[r, :, cols], key_rows[r, :, cols], values[r, :, cols]
            gcol, grow, glast = gsum_cols[:, h : h + 1], gsum_rows[h : h + 1], last[h : h + 1]
            gap = jnp.where(causal, jnp.exp(jnp.minimum(gcol - grow, 0.0)), 0.0)
            weights = (nt(q, k) * gap).astype(BF16)
            heads[r, :, cols] = jnp.dot(weights, v, preferred_element_type=F32)
            weighted = (k.astype(F32) * jnp.exp(glast - gcol)).astype(BF16)
            kv[r, h * size : (h + 1) * size, :] = tn(weighted, v)
            decay_cols[r, :, cols] = jnp.broadcast_to(grown[:, h : h + 1], (length, size))
        return carry

    lax.fori_loop(0, count, block, 0)

    @pl.when(me == last)
    def _():
        each_z(lambda p: signal(barrier, (me, p)))

    own_kv_copy = fetch(strip(kv, me), part(kv_pieces, me), 13)

    each_peer(lambda p: kv_copy(p).start())

    await_all(slots, slot_recv, others)
    await_all(decays, decay_recv, others)
    for copy in [fetch(slots, slots_s, 9), fetch(decays, decays_s, 10)]:
        copy.wait()
    place = (
        lax.broadcasted_iota(jnp.int32, (8, LANES), 0) * LANES
        + lax.broadcasted_iota(jnp.int32, (8, LANES), 1)
    )
    my_head = (me * rows) // size

    def invert(device, found):
        hit_row, kv_row, decay = found
        for r in range(count):
            here = place == slots_s[device, 0, WRITE + r]
            hit_row = jnp.where(here, slots_s[device, 0, HIT + r], hit_row)
            kv_row = jnp.where(here, device * count + r, kv_row)
            decay = jnp.where(here, decays_s[device, 0, r * head_count + my_head], decay)
        return hit_row, kv_row, decay

    hit_row, kv_row, decay = lax.fori_loop(
        0, n, invert, (place, jnp.full((8, LANES), none, jnp.int32), jnp.ones((8, LANES), F32))
    )
    source_rows[0] = hit_row
    source_rows[1] = kv_row
    source_decay[...] = decay
    sources_in = [fetch(source_rows, source_rows_s, 11), fetch(source_decay, source_decay_s, 12)]


    own_cache_copy.wait()
    await_all(pieces, cache_recv, other_pieces)

    def pick(device):
        for r in range(count):
            hit_pieces[device * count + r] = pieces[slots_s[device, 0, HIT + r]]

    def send_hits(p):
        pick(p)
        hit_copy(p).start()

    each_peer(send_hits)
    pick(me)
    own_hit_copy = fetch(part(hit_pieces, me), strip(prefix, me), 14)

    @pl.when(me == last)
    def _():
        pl.semaphore_wait(barrier, nz - 1)
        each_peer(lambda p: signal(planes_in, (p, z)))

    own_kv_copy.wait()
    await_all(kv_pieces, kv_recv, other_pieces)
    for copy in sources_in:
        copy.wait()

    def renew(device):
        for e in range(count):
            slot = device * count + e
            sub, at = lax.div(slot, LANES), lax.rem(slot, LANES)
            state = source_decay_s[sub, at] * pieces[source_rows_s[0, sub, at]]
            new_pieces[slot] = state + kv_pieces[source_rows_s[1, sub, at]]

    def send_new(p):
        renew(p)
        new_copy(p).start()

    each_peer(send_new)
    renew(me)
    own_new_copy = fetch(part(new_pieces, me), strip(new_cache, me), 15)

    own_hit_copy.wait()
    await_all(hit_pieces, hit_recv, other_pieces)
    lane_wide = lax.broadcasted_iota(jnp.int32, (length, LANES), 1)

    def carry_in(r, sums):
        total = jnp.zeros((length, 1), F32)
        for h in range(head_count):
            cols = slice(h * size, (h + 1) * size)
            state = prefix[r, h * size : (h + 1) * size, :]
            state_high = state.astype(BF16)
            state_low = (state - state_high.astype(F32)).astype(BF16)
            q = queries[r, :, cols]
            carried = jnp.dot(q, state_high, preferred_element_type=F32)
            carried = carried + jnp.dot(q, state_low, preferred_element_type=F32)
            out = heads[r, :, cols] + carried * decay_cols[r, :, cols]
            heads[r, :, cols] = out
            total = total + jnp.sum(out * out, axis=1, keepdims=True)
        return jnp.where(lane_wide == r, total, sums)

    sums = lax.fori_loop(0, count, carry_in, jnp.zeros((length, LANES), F32), unroll=UNROLL)
    flat = jnp.transpose(sums)
    packed = jnp.concatenate([flat[0:8], flat[8:16]], axis=1)
    own_squares[...] = packed
    squares[z] = packed

    @pl.when(me != last)
    def _():
        pl.semaphore_wait(planes_in, 1)

    each_z(lambda p: square_copy(p).start())
    await_all(squares, square_recv, nz - 1)
    total = jnp.sum(squares[...], axis=0)
    inv = lax.rsqrt(total / (width * nz) + 1e-06)
    inv = jnp.transpose(inv)

    wide_gain = jnp.broadcast_to(gain[...], (length, width))
    for r in range(count):
        down, at = (r // 8) * length, r % 8
        scale = jnp.broadcast_to(inv[down : down + length, at : at + 1], (length, width))
        attended[r] = (heads[r] * scale * wide_gain).astype(BF16)

    own_new_copy.wait()
    await_all(new_pieces, new_recv, other_pieces)
    await_all(slots, slot_send, others)
    await_all(decays, decay_send, others)
    await_all(new_pieces, new_send, other_pieces)
    await_all(pieces, cache_send, other_pieces)
    await_all(kv_pieces, kv_send, other_pieces)
    await_all(hit_pieces, hit_send, other_pieces)
    await_all(squares, square_send, nz - 1)


def write_out(attended, new_cache, attended_out, new_cache_out, done):
    quarter = new_cache.shape[0] // 4
    copies = [pltpu.make_async_copy(attended, attended_out, done.at[4])]
    for k in range(4):
        part = pl.ds(k * quarter, quarter)
        copies.append(pltpu.make_async_copy(new_cache.at[part], new_cache_out.at[part], done.at[k]))
    for copy in copies:
        copy.start()
    for copy in copies:
        copy.wait()


def body(
    n, nz, queries, key_rows, values, log_decay, state_cache, norm_gain, entry_slot, hit_entry, write_entry
):
    count, length, width = queries.shape
    entries, head_count, size, _ = state_cache.shape
    tall = head_count * size
    rows = tall // n
    vmem, hbm = pl.BlockSpec(memory_space=pltpu.VMEM), pl.BlockSpec(memory_space=pltpu.HBM)
    sem = pltpu.SemaphoreType.DMA
    attended, new_cache = pl.pallas_call(
        functools.partial(kernel, n, nz),
        out_shape=(
            pltpu.VMEM((count, length, width), BF16),
            pltpu.VMEM((entries, tall, size), F32),
        ),
        in_specs=[hbm] * 9,
        out_specs=(vmem, vmem),
        scratch_shapes=[
            pltpu.VMEM((n * entries + 8, rows, size), F32),
            pltpu.VMEM((n * count + 8, rows, size), F32),
            pltpu.VMEM((count, tall, size), F32),
            pltpu.VMEM((n * count, rows, size), F32),
            pltpu.VMEM((n * entries, rows, size), F32),
            pltpu.VMEM((count, tall, size), F32),
            pltpu.VMEM((count, length, width), F32),
            pltpu.VMEM((count, length, width), F32),
            pltpu.VMEM((1, LANES), jnp.int32),
            pltpu.VMEM((n, 1, LANES), jnp.int32),
            pltpu.VMEM((1, LANES), F32),
            pltpu.VMEM((n, 1, LANES), F32),
            pltpu.VMEM((2, 8, LANES), jnp.int32),
            pltpu.VMEM((8, LANES), F32),
            pltpu.VMEM((8, LANES), F32),
            pltpu.VMEM((nz, 8, LANES), F32),
            pltpu.VMEM(log_decay.shape, F32),
            *[pltpu.VMEM((count, length, width), BF16)] * 3,
            pltpu.VMEM((1, width), F32),
            pltpu.SMEM((n, 1, LANES), jnp.int32),
            pltpu.SMEM((n, 1, LANES), F32),
            pltpu.SMEM((2, 8, LANES), jnp.int32),
            pltpu.SMEM((8, LANES), F32),
            pltpu.SMEM(entry_slot.shape, jnp.int32),
            pltpu.SMEM(hit_entry.shape, jnp.int32),
            pltpu.SMEM(write_entry.shape, jnp.int32),
            *[sem] * 14,
            sem((16,)),
            *[pltpu.SemaphoreType.REGULAR] * 3,
        ],
        compiler_params=pltpu.CompilerParams(
            collective_id=0, has_side_effects=True, vmem_limit_bytes=32 << 20
        ),
    )(
        *(
            pltpu.with_memory_space_constraint(x, pltpu.HBM)
            for x in (
                entry_slot, hit_entry, write_entry, log_decay, queries, key_rows, values,
                norm_gain.reshape(1, width), state_cache.reshape(entries, tall, size),
            )
        )
    )
    attended, new_cache = pl.pallas_call(
        write_out,
        out_shape=(
            jax.ShapeDtypeStruct((count, length, width), BF16),
            jax.ShapeDtypeStruct((entries, tall, size), F32),
        ),
        in_specs=[vmem, vmem],
        out_specs=(pl.BlockSpec(memory_space=pl.ANY),) * 2,
        scratch_shapes=[sem((5,))],
    )(*(pltpu.with_memory_space_constraint(a, pltpu.VMEM) for a in (attended, new_cache)))
    return attended, new_cache.reshape(state_cache.shape)


def solution(mesh):
    placed = (
        P("req", None, "head"),
        P("req", None, "head"),
        P("req", None, "head"),
        P("req", "head", None),
        P("req", "head", None, None),
        P("head"),
        P(),
        P("req"),
        P("req"),
    )
    return jax.shard_map(
        functools.partial(body, mesh.shape["req"], mesh.shape["head"]),
        mesh=mesh,
        in_specs=placed,
        out_specs=(P("req", None, "head"), P("req", "head", None, None)),
        check_vma=False,
    )
```
